32 devices in a mesh: dp: 8 (over z, x), fsdp: 4 (over y, core).
Axes of the slice: x: 2, y: 2, z: 4, core: 2. Of those that a mesh axis runs over, the one named last changes fastest.
Arguments:
- tokens: bfloat16 [32, 128, 2048], P(('dp', 'fsdp')), may hold values from -6 to 6
- patches: bfloat16 [32, 256, 1664], P(('dp', 'fsdp')), may hold values from -6 to 6
- cotangent: bfloat16 [32, 128, 2048], P(('dp', 'fsdp')), may hold values from -6 to 6
- lengths: int32 [32], P(('dp', 'fsdp')), may hold values from 8 to 128, as said below
- episode_flags: int32 [32], P(('dp', 'fsdp')), may hold values 0 or 1
- norm_gains: float32 [3, 2048], replicated, may hold values from 0.1 to 1.9
- w_query: bfloat16 [2048, 2048], P('fsdp'), may hold values from -0.125 to 0.125
- w_key: bfloat16 [2048, 2048], P('fsdp'), may hold values from -0.125 to 0.125
- w_value: bfloat16 [2048, 2048], P('fsdp'), may hold values from -0.125 to 0.125
- w_out: bfloat16 [2048, 2048], P('fsdp'), may hold values from -0.375 to 0.375
- c_query: bfloat16 [2048, 2048], P('fsdp'), may hold values from -0.125 to 0.125
- c_key: bfloat16 [2048, 2048], P('fsdp'), may hold values from -0.125 to 0.125
- c_value: bfloat16 [2048, 2048], P('fsdp'), may hold values from -0.125 to 0.125
- c_out: bfloat16 [2048, 2048], P('fsdp'), may hold values from -0.5 to 0.5
- patch_proj: bfloat16 [1664, 2048], P('fsdp'), may hold values from -0.15625 to 0.15625
- w_gate: bfloat16 [5120, 2048], P('fsdp'), may hold values from -0.125 to 0.125
- w_up: bfloat16 [5120, 2048], P('fsdp'), may hold values from -0.125 to 0.125
- w_down: bfloat16 [5120, 2048], P('fsdp'), may hold values from -0.078125 to 0.078125
Outputs:
- out_tokens: bfloat16 [32, 128, 2048], P(('dp', 'fsdp'))
- tokens_grad: float32 [32, 128, 2048], P(('dp', 'fsdp'))
- patches_grad: float32 [32, 256, 1664], P(('dp', 'fsdp'))
- gains_grad: float32 [3, 2048], replicated
- w_query_grad: float32 [2048, 2048], P('fsdp', 'dp')
- w_key_grad: float32 [2048, 2048], P('fsdp', 'dp')
- w_value_grad: float32 [2048, 2048], P('fsdp', 'dp')
- w_out_grad: float32 [2048, 2048], P('fsdp', 'dp')
- c_query_grad: float32 [2048, 2048], P('fsdp', 'dp')
- c_key_grad: float32 [2048, 2048], P('fsdp', 'dp')
- c_value_grad: float32 [2048, 2048], P('fsdp', 'dp')
- c_out_grad: float32 [2048, 2048], P('fsdp', 'dp')
- patch_proj_grad: float32 [1664, 2048], P('fsdp', 'dp')
- w_gate_grad: float32 [5120, 2048], P('fsdp', 'dp')
- w_up_grad: float32 [5120, 2048], P('fsdp', 'dp')
- w_down_grad: float32 [5120, 2048], P('fsdp', 'dp')
The draws below stay inside these ranges and needn't reach their ends.
Inputs may be any that keep to these rules, and one draw needn't show every extreme that they name: `lengths`: text length of each sequence; some sequence has length 128 and some 128 // 16. `episode_flags`: 1 marks a robot episode (causal attention), 0 a caption pair (its first half of tokens attends both ways).
All inputs are finite; a program needn't handle non-finite values. No bound on the sum of `episode_flags` on one device may be relied on, other than what follows from the above.
Results may differ from the reference program's by a relative error of at most 0.028.
Values may be sent and summed in bfloat16 or wider, within the bound.
No kernel may reach another device: no remote copies, remote signals or barrier semaphores. Data moves between devices by JAX's collectives and lax.ppermute only.
A program may use at most 640 MiB of HBM per device.

```python
import math
import jax
import jax.numpy as jnp
from jax import lax

D = 2048
H = 16
HD = 128
FF = 5120
VD = 1664
P_SIZE = 256
SLOT = 128
SEQS = 32


def draw_lengths(key, part):
    key = jax.random.fold_in(key, 11)
    pick_key, spot_key = jax.random.split(key)
    drawn = jax.random.randint(pick_key, (SEQS,), SLOT // 16, SLOT + 1)
    spot = jax.random.randint(spot_key, (), 0, SEQS)
    drawn = drawn.at[spot].set(SLOT)
    drawn = drawn.at[(spot + 1) % SEQS].set(SLOT // 16)
    return drawn.astype(jnp.int32)


def set_ends(values, own_key, low, top_value):
    extent = values.shape
    spot = [jax.random.randint(jax.random.fold_in(own_key, axis), (), 0, extent[axis]) for axis in range(len(extent))]
    values = values.at[tuple(spot)].set(low)
    longest = extent.index(max(extent))
    spot[longest] = (spot[longest] + 1) % extent[longest]
    return values.at[tuple(spot)].set(top_value)


def levels(own_key, extent, pieces, low, top_value):
    def one(position, shards_of):
        draws = jax.random.uniform(jax.random.fold_in(jax.random.fold_in(own_key, 6), position), (shards_of,), jnp.float32, low / len(pieces), top_value / len(pieces))
        return jnp.repeat(jnp.exp(draws), extent[position] // shards_of).reshape((-1,) + (1,) * (len(extent) - position - 1))

    loudness = one(*pieces[0])
    for cut in pieces[1:]:
        loudness = loudness * one(*cut)
    return loudness


def scatter_about(rng, extent, width, limit, shards=(), kind=jnp.bfloat16):
    values = width * jax.random.normal(rng, extent, jnp.float32)
    if shards:
        values = values * levels(rng, extent, shards, -0.22, 0.18)
    return jnp.clip(values, -limit, limit).astype(kind)


def setup_inputs(seed: int = 0) -> dict:
    seeds = jax.random.split(jax.random.key(seed), 19)
    tokens = scatter_about(seeds[0], (SEQS, SLOT, D), 1.0, 6.0, ((0, 32),))
    patches = scatter_about(seeds[1], (SEQS, P_SIZE, VD), 1.0, 6.0, ((0, 32),))
    cotangent = scatter_about(seeds[2], (SEQS, SLOT, D), 1.0, 6.0, ((0, 32),))
    lengths = draw_lengths(jax.random.fold_in(seeds[18], 71), 0)
    episode_flags = set_ends((jax.random.randint(seeds[4], (SEQS,), 0, 2) < 1).astype(jnp.int32), jax.random.fold_in(seeds[4], 1), 0, 1)
    norm_gains = jnp.clip(1.0 + 0.18 * jax.random.normal(seeds[5], (3, D), jnp.float32), 0.1, 1.9)
    w_query = scatter_about(seeds[6], (D, D), D ** -0.5, 0.125, ((0, 4),))
    w_key = scatter_about(seeds[7], (D, D), D ** -0.5, 0.125, ((0, 4),))
    w_value = scatter_about(seeds[8], (D, D), D ** -0.5, 0.125, ((0, 4),))
    w_out = scatter_about(seeds[9], (D, D), (D // 8) ** -0.5, 0.375, ((0, 4),))
    c_query = scatter_about(seeds[10], (D, D), D ** -0.5, 0.125, ((0, 4),))
    c_key = scatter_about(seeds[11], (D, D), D ** -0.5, 0.125, ((0, 4),))
    c_value = scatter_about(seeds[12], (D, D), D ** -0.5, 0.125, ((0, 4),))
    c_out = scatter_about(seeds[13], (D, D), (D // 16) ** -0.5, 0.5, ((0, 4),))
    patch_proj = scatter_about(seeds[14], (VD, D), VD ** -0.5, 0.15625, ((0, 4),))
    w_gate = scatter_about(seeds[15], (FF, D), D ** -0.5, 0.125, ((0, 4),))
    w_up = scatter_about(seeds[16], (FF, D), D ** -0.5, 0.125, ((0, 4),))
    w_down = scatter_about(seeds[17], (FF, D), FF ** -0.5, 0.078125, ((0, 4),))
    return {"tokens": tokens, "patches": patches, "cotangent": cotangent, "lengths": lengths, "episode_flags": episode_flags, "norm_gains": norm_gains, "w_query": w_query, "w_key": w_key, "w_value": w_value, "w_out": w_out, "c_query": c_query, "c_key": c_key, "c_value": c_value, "c_out": c_out, "patch_proj": patch_proj, "w_gate": w_gate, "w_up": w_up, "w_down": w_down}


@jax.custom_vjp
def low(v):
    return lax.optimization_barrier(v.astype(jnp.bfloat16)).astype(jnp.float32)

@jax.custom_vjp
def low_back(v):
    return v

def low_keep(v):
    return (low(v), None)

def low_pass(kept, grad):
    return (grad,)

def back_keep(v):
    return (v, None)

def back_low(kept, grad):
    return (low(grad),)
low.defvjp(low_keep, low_pass)
low_back.defvjp(back_keep, back_low)

def round_both(value):
    return low(low_back(value))

def matmul_high(left, right):
    return jnp.dot(left, right, precision=lax.Precision.HIGHEST, preferred_element_type=jnp.float32)

def normed(values, gain):
    return values * lax.rsqrt(lax.optimization_barrier(jnp.mean(values * values, axis=-1, keepdims=True)) + 1e-06) * gain

def mask_tables(lengths, episode_flags, slot_len):
    positions = jnp.arange(slot_len, dtype=jnp.int32)
    bucket_len = jnp.where(lengths <= slot_len // 4, slot_len // 4, jnp.where(lengths <= slot_len // 2, slot_len // 2, slot_len))
    prefix_len = jnp.where(episode_flags == 0, lengths // 2, 0)
    query_pos = positions[None, :, None]
    key_pos = positions[None, None, :]
    allowed = (key_pos < lengths[:, None, None]) & ((key_pos <= query_pos) | (key_pos < prefix_len[:, None, None]))
    live_rows = (positions[None, :] < bucket_len[:, None]).astype(jnp.float32)[:, :, None]
    return (allowed, live_rows)

def attention(queries, keys, values, allowed):
    seq_count = queries.shape[0]
    query_heads = queries.reshape(seq_count, queries.shape[1], H, HD)
    key_heads = keys.reshape(seq_count, keys.shape[1], H, HD)
    value_heads = values.reshape(seq_count, values.shape[1], H, HD)
    scores = jnp.einsum('gqhd,gkhd->ghqk', query_heads, key_heads, precision=lax.Precision.HIGHEST) * HD ** (-0.5)
    scores = low_back(scores)
    if allowed is not None:
        scores = jnp.where(allowed[:, None], scores, -1e+30)
    row_max = lax.optimization_barrier(jnp.max(scores, axis=-1, keepdims=True))
    weights = jnp.exp(scores - row_max)
    probs = low(weights / lax.optimization_barrier(jnp.sum(weights, axis=-1, keepdims=True)))
    mixed = jnp.einsum('ghqk,gkhd->gqhd', probs, value_heads, precision=lax.Precision.HIGHEST)
    return mixed.reshape(seq_count, queries.shape[1], H * HD)

def layer(tokens, patches, gains, w_query, w_key, w_value, w_out, c_query, c_key, c_value, c_out, patch_proj, w_gate, w_up, w_down, allowed, live_rows):
    first = low(normed(tokens, gains[0]))
    queries = round_both(matmul_high(first, w_query))
    keys = round_both(matmul_high(first, w_key))
    values = round_both(matmul_high(first, w_value))
    self_mixed = round_both(attention(queries, keys, values, allowed))
    after_self = tokens + low_back(matmul_high(self_mixed, w_out))
    second = low(normed(after_self, gains[1]))
    cross_queries = round_both(matmul_high(second, c_query))
    context = round_both(matmul_high(patches, patch_proj))
    cross_keys = round_both(matmul_high(context, c_key))
    cross_values = round_both(matmul_high(context, c_value))
    cross_mixed = round_both(attention(cross_queries, cross_keys, cross_values, None))
    after_cross = after_self + low_back(matmul_high(cross_mixed, c_out))
    third = low(normed(after_cross, gains[2]))
    gate_value = low_back(matmul_high(third, w_gate.T))
    up_value = low_back(matmul_high(third, w_up.T))
    hidden = low(jax.nn.gelu(gate_value, approximate=True) * up_value)
    return (after_cross + low_back(matmul_high(hidden, w_down))) * live_rows

def reference(tokens, patches, cotangent, lengths, episode_flags, norm_gains, w_query, w_key, w_value, w_out, c_query, c_key, c_value, c_out, patch_proj, w_gate, w_up, w_down):
    seq_total = tokens.shape[0]
    group_size = math.gcd(seq_total, 32)
    group_count = seq_total // group_size
    matrices = tuple((weight.astype(jnp.float32) for weight in (w_query, w_key, w_value, w_out, c_query, c_key, c_value, c_out, patch_proj, w_gate, w_up, w_down)))

    def shaped(array):
        return array.reshape((group_count, group_size) + array.shape[1:])

    def one_group(carry, block):
        tok_block, patch_block, cot_block, length_block, flag_block = block
        allowed, live_rows = mask_tables(length_block, flag_block, tok_block.shape[1])

        def forward(tok_in, patch_in, gains, *weight_list):
            return layer(tok_in, patch_in, gains, *weight_list, allowed, live_rows)
        result, pull = jax.vjp(forward, tok_block.astype(jnp.float32), patch_block.astype(jnp.float32), norm_gains, *matrices)
        grads = pull(cot_block.astype(jnp.float32))
        new_carry = tuple((old_sum + new_term for old_sum, new_term in zip(carry, grads[2:])))
        return (new_carry, (result.astype(jnp.bfloat16), grads[0], grads[1]))
    start = tuple((jnp.zeros(weight.shape, jnp.float32) for weight in (norm_gains,) + matrices))
    final, stacked = lax.scan(one_group, start, (shaped(tokens), shaped(patches), shaped(cotangent), shaped(lengths), shaped(episode_flags)))
    out_tokens = stacked[0].reshape(tokens.shape)
    tokens_grad = stacked[1].reshape(tokens.shape)
    patches_grad = stacked[2].reshape(patches.shape)
    return (out_tokens, tokens_grad, patches_grad, final[0], final[1], final[2], final[3], final[4], final[5], final[6], final[7], final[8], final[9], final[10], final[11], final[12])
```

```python
import functools

import jax
import jax.numpy as jnp
from jax import lax
from jax.experimental import pallas as pl
from jax.experimental.pallas import tpu as pltpu
from jax.sharding import PartitionSpec as P

HD = 128
SCALE = HD ** (-0.5)
EPS = 1e-06
BF = jnp.bfloat16
F32 = jnp.float32
GROUP = 4


def cost(us):
    return pl.CostEstimate(
        flops=int(us * 8e8), bytes_accessed=int(us * 2e6), transcendentals=0
    )


def low(v):
    return v.astype(BF)


def dot(left, right, left_dim, right_dim):
    return lax.dot_general(
        left, right, (((left_dim,), (right_dim,)), ((), ())), preferred_element_type=F32
    )


def nn(left, right):
    return dot(left, right, 1, 0)


def nt(left, right):
    return dot(left, right, 1, 1)


def tn(left, right):
    return dot(left, right, 0, 0)


def normed(values, gain):
    return low(values * lax.rsqrt(jnp.mean(values * values, axis=-1, keepdims=True) + EPS) * gain)


def norm_back(values, gain, grad):
    scale = lax.rsqrt(jnp.mean(values * values, axis=-1, keepdims=True) + EPS)
    unit = values * scale
    weighted = grad * gain
    grad_values = scale * (weighted - unit * jnp.mean(weighted * unit, axis=-1, keepdims=True))
    return grad_values, jnp.sum(grad * unit, axis=0)


def gelu_parts(v):
    c = 0.7978845608028654
    t = jnp.tanh(c * (v + 0.044715 * (v * v * v)))
    value = 0.5 * v * (1.0 + t)
    slope = 0.5 * (1.0 + t) + 0.5 * v * (1.0 - t * t) * (c * (1.0 + 3 * 0.044715 * v * v))
    return value, slope


def allowed_at(info, rows, columns):
    length = info[pl.program_id(0), 0]
    flag = info[pl.program_id(0), 1]
    prefix = jnp.where(flag == 0, length // 2, 0)
    query = lax.broadcasted_iota(jnp.int32, (rows, columns), 0)
    key = lax.broadcasted_iota(jnp.int32, (rows, columns), 1)
    return (key < length) & ((key <= query) | (key < prefix))


def probabilities(q, k, allowed):
    scores = nt(q, k) * SCALE
    if allowed is not None:
        scores = jnp.where(allowed, scores, -1e30)
    weights = jnp.exp(scores - jnp.max(scores, axis=-1, keepdims=True))
    return weights / jnp.sum(weights, axis=-1, keepdims=True)


def attend_kernel(masked, info, q_ref, k_ref, v_ref, out_ref):
    allowed = allowed_at(info, q_ref.shape[0], k_ref.shape[0]) if masked else None
    for head in range(q_ref.shape[1] // HD):
        at = pl.ds(head * HD, HD)
        probs = probabilities(q_ref[:, at], k_ref[:, at], allowed)
        out_ref[:, at] = low(nn(low(probs), v_ref[:, at]))


def attend_back_kernel(masked, info, q_ref, k_ref, v_ref, g_ref, gq_ref, gk_ref, gv_ref):
    allowed = allowed_at(info, q_ref.shape[0], k_ref.shape[0]) if masked else None
    for head in range(q_ref.shape[1] // HD):
        at = pl.ds(head * HD, HD)
        q, k, v, g = q_ref[:, at], k_ref[:, at], v_ref[:, at], g_ref[:, at]
        probs = probabilities(q, k, allowed)
        grad_probs = nt(g, v)
        gv_ref[:, at] = low(tn(low(probs), g))
        total = jnp.sum(probs * grad_probs, axis=-1, keepdims=True)
        grad_scores = low(probs * (grad_probs - total))
        gq_ref[:, at] = low(nn(grad_scores, k) * SCALE)
        gk_ref[:, at] = low(tn(grad_scores, q) * SCALE)


def head_block(rows, width):
    return pl.BlockSpec((rows, width), lambda s, info: (s, 0))


def attend(info, q, k, v, rows, keys, width, masked):
    return pl.pallas_call(
        functools.partial(attend_kernel, masked),
        out_shape=jax.ShapeDtypeStruct((GROUP * rows, width), BF),
        grid_spec=pltpu.PrefetchScalarGridSpec(
            num_scalar_prefetch=1,
            grid=(GROUP,),
            in_specs=[
                head_block(rows, width),
                head_block(keys, width),
                head_block(keys, width),
            ],
            out_specs=head_block(rows, width),
        ),
        compiler_params=pltpu.CompilerParams(vmem_limit_bytes=24 << 20),
        cost_estimate=cost(6 if masked else 4),
    )(info, q, k, v)


def attend_back(info, q, k, v, grad, rows, keys, width, masked):
    return pl.pallas_call(
        functools.partial(attend_back_kernel, masked),
        out_shape=(
            jax.ShapeDtypeStruct((GROUP * rows, width), BF),
            jax.ShapeDtypeStruct((GROUP * keys, width), BF),
            jax.ShapeDtypeStruct((GROUP * keys, width), BF),
        ),
        grid_spec=pltpu.PrefetchScalarGridSpec(
            num_scalar_prefetch=1,
            grid=(GROUP,),
            in_specs=[
                head_block(rows, width),
                head_block(keys, width),
                head_block(keys, width),
                head_block(rows, width),
            ],
            out_specs=(
                head_block(rows, width),
                head_block(keys, width),
                head_block(keys, width),
            ),
        ),
        compiler_params=pltpu.CompilerParams(vmem_limit_bytes=24 << 20),
        cost_estimate=cost(8),
    )(info, q, k, v, grad)


def placed(place, pieces):
    rows = pieces[0].shape[0]
    half = rows // 2
    f, x = place[0], place[1] % 2

    def at(block, part):
        return pl.multiple_of((f ^ block) * rows + part * half, half)

    spots = (
        pl.ds(at(0, 0), rows),
        pl.ds(at(1, 0), rows),
        pl.ds(at(2, x), half),
        pl.ds(at(2, 1 - x), half),
        pl.ds(at(3, x), half),
        pl.ds(at(3, 1 - x), half),
    )
    return tuple(zip(pieces, spots))


def row_tiles(rows, body):
    size = next((size for size in (512, 640) if rows % size == 0), rows)
    if size == rows:
        body(pl.ds(0, rows))
    else:
        pl.loop(0, rows // size)(lambda i: body(pl.ds(pl.multiple_of(i * size, size), size)))


def to_heads_kernel(count, place, *refs):
    pieces, out_ref = placed(place, refs[count : count + 6]), refs[count + 6]
    start = 0
    for rows_ref in refs[:count]:
        total = None
        for piece, features in pieces:
            term = nn(rows_ref[:, features], piece[...])
            total = term if total is None else total + term
        out_ref[pl.ds(start, rows_ref.shape[0]), :] = low(total)
        start += rows_ref.shape[0]


def from_heads_kernel(count, place, *refs):
    grads, pieces, out_ref = refs[:count], refs[count:-1], refs[-1]

    def tile(at):
        for part in range(6):
            total = None
            for i in range(count):
                piece, features = placed(place, pieces[6 * i : 6 * i + 6])[part]
                term = nt(grads[i][at, :], piece[...])
                total = term if total is None else total + term
            out_ref[at, features] = low(total)

    row_tiles(out_ref.shape[0], tile)


def piece_specs(pieces):
    rows, width = pieces[0].shape[0], pieces[1][0].shape[-1]
    specs = [pl.BlockSpec((rows, width), lambda i, place: (0, place[0]))]
    for array, at in pieces[1:]:
        block = (None,) * len(at) + array.shape[len(at) :]
        specs.append(pl.BlockSpec(block, lambda i, place, at=at: (*at, 0, 0)))
    return specs


def piece_arrays(pieces):
    return [pieces[0]] + [array for array, at in pieces[1:]]


def fixed(array):
    return pl.BlockSpec(array.shape, lambda i, place: (0, 0))


def to_heads(place, blocks, pieces):
    out = (sum(block.shape[0] for block in blocks), pieces[1][0].shape[-1])
    return pl.pallas_call(
        functools.partial(to_heads_kernel, len(blocks)),
        out_shape=jax.ShapeDtypeStruct(out, BF),
        grid_spec=pltpu.PrefetchScalarGridSpec(
            num_scalar_prefetch=1,
            grid=(1,),
            in_specs=[fixed(block) for block in blocks] + piece_specs(pieces),
            out_specs=pl.BlockSpec(out, lambda i, place: (0, 0)),
        ),
        compiler_params=pltpu.CompilerParams(vmem_limit_bytes=48 << 20),
        cost_estimate=cost(out[0] / 190),
    )(place, *blocks, *piece_arrays(pieces))


def from_heads(place, grads, weights):
    count = len(weights)
    out = (grads[0].shape[0], weights[0][0].shape[1])
    specs = [spec for pieces in weights for spec in piece_specs(pieces)]
    return pl.pallas_call(
        functools.partial(from_heads_kernel, count),
        out_shape=jax.ShapeDtypeStruct(out, BF),
        grid_spec=pltpu.PrefetchScalarGridSpec(
            num_scalar_prefetch=1,
            grid=(1,),
            in_specs=[fixed(g) for g in grads] + specs,
            out_specs=pl.BlockSpec(out, lambda i, place: (0, 0)),
        ),
        compiler_params=pltpu.CompilerParams(vmem_limit_bytes=56 << 20),
        cost_estimate=cost(3 + out[0] * count / 230),
    )(place, *grads, *[array for pieces in weights for array in piece_arrays(pieces)])


def half_kernel(place, *refs):
    lefts, rights, out_ref = refs[0:-1:2], refs[1:-1:2], refs[-1]
    start = 0
    for left, right in zip(lefts, rights):

        def product(at, start=start, left=left, right=right):
            out_ref[0, pl.ds(pl.multiple_of(start + at.start, 16), at.size), :] = low(
                nn(left[at, :], right[...])
            )

        row_tiles(left.shape[0], product)
        start += left.shape[0]


def half_grads(place, terms, order, side):
    def target(k, place):
        rel = (side << order[0]) + ((k // 2) << order[1]) + ((k % 2) << order[2])
        return place[1] ^ rel

    def source(k, place):
        return (target(k, place) // 2) ^ place[0]

    specs, arrays = [], []
    rows = 0
    for kind, left, right in terms:
        tall, tokens = left.shape[-2:]
        if kind == "columns":
            tall, wide = tall // GROUP, right.shape[1] // 2
            specs.append(pl.BlockSpec((tall, tokens), lambda k, place: (target(k, place) // 2, 0)))
            specs.append(pl.BlockSpec((tokens, wide), lambda k, place: (0, target(k, place) % 2)))
        elif kind == "owners":
            right, column = right
            wide = left.shape[-2] // 2
            specs.append(
                pl.BlockSpec((None, tall, tokens), lambda k, place: (source(k, place), 0, 0))
            )
            specs.append(
                pl.BlockSpec(
                    (None, tokens, wide),
                    lambda k, place, column=column: (
                        source(k, place),
                        0,
                        2 * column + target(k, place) % 2,
                    ),
                )
            )
        else:
            wide = right.shape[1] // 8
            specs.append(pl.BlockSpec((tall, tokens), lambda k, place: (0, 0)))
            specs.append(pl.BlockSpec((tokens, wide), lambda k, place: (0, target(k, place))))
        arrays += [left, right]
        rows += tall
    return pl.pallas_call(
        half_kernel,
        out_shape=jax.ShapeDtypeStruct((4, rows, wide), BF),
        grid_spec=pltpu.PrefetchScalarGridSpec(
            num_scalar_prefetch=1,
            grid=(4,),
            in_specs=specs,
            out_specs=pl.BlockSpec((1, rows, wide), lambda k, place: (k, 0, 0)),
        ),
        compiler_params=pltpu.CompilerParams(vmem_limit_bytes=48 << 20),
        cost_estimate=cost(rows / 210),
    )(place, *arrays)


def turn_kernel(*refs):
    start = 0
    for block in refs[:-1]:
        rows = block.shape[0]
        refs[-1][:, pl.ds(start, rows)] = block[...].T
        start += rows


def turn(*blocks):
    width = blocks[0].shape[1]
    step = 512 if width % 512 == 0 else width
    rows = sum(block.shape[0] for block in blocks)
    return pl.pallas_call(
        turn_kernel,
        out_shape=jax.ShapeDtypeStruct((width, rows), BF),
        grid=(width // step,),
        in_specs=[pl.BlockSpec((block.shape[0], step), lambda i: (0, i)) for block in blocks],
        out_specs=pl.BlockSpec((step, rows), lambda i: (i, 0)),
        compiler_params=pltpu.CompilerParams(vmem_limit_bytes=32 << 20),
        cost_estimate=cost(3),
    )(*blocks)


def turn_own_kernel(place, *refs):
    blocks, out_ref = refs[:-1], refs[-1]
    rows = blocks[0].shape[0]
    for k, block in enumerate(blocks):
        turned = block[...].T
        for r in range(GROUP):
            out_ref[r, :, pl.ds((k ^ r) * rows, rows)] = turned


def turn_own(place, blocks, width):
    rows = blocks[0].shape[0]
    out = (GROUP, width, GROUP * rows)
    return pl.pallas_call(
        turn_own_kernel,
        out_shape=jax.ShapeDtypeStruct(out, BF),
        grid_spec=pltpu.PrefetchScalarGridSpec(
            num_scalar_prefetch=1,
            grid=(1,),
            in_specs=[pl.BlockSpec((rows, width), lambda i, place: (0, place[0]))] * GROUP,
            out_specs=pl.BlockSpec(out, lambda i, place: (0, 0, 0)),
        ),
        compiler_params=pltpu.CompilerParams(vmem_limit_bytes=32 << 20),
        cost_estimate=cost(3),
    )(place, *blocks)


def join_kernel(place, *refs):
    for r, block in enumerate(refs[:-1]):

        @pl.when(pl.program_id(0) == r)
        def _():
            refs[-1][...] = block[...]


def join(place, blocks):
    rows, width = blocks[0].shape
    return pl.pallas_call(
        join_kernel,
        out_shape=jax.ShapeDtypeStruct((GROUP * rows, width), BF),
        grid_spec=pltpu.PrefetchScalarGridSpec(
            num_scalar_prefetch=1,
            grid=(GROUP,),
            in_specs=[fixed(block) for block in blocks],
            out_specs=pl.BlockSpec((rows, width), lambda i, place: (place[0] ^ i, 0)),
        ),
        compiler_params=pltpu.CompilerParams(vmem_limit_bytes=40 << 20),
        cost_estimate=cost(5),
    )(place, *blocks)


def all_grads(parts, terms):
    rows = sum(left.shape[0] for left, right in terms)
    wide = terms[0][1].shape[1] // parts
    specs = []
    for left, right in terms:
        specs.append(pl.BlockSpec(left.shape, lambda p, place: (0, 0)))
        specs.append(pl.BlockSpec((right.shape[0], wide), lambda p, place: (0, p)))
    return pl.pallas_call(
        half_kernel,
        out_shape=jax.ShapeDtypeStruct((parts, rows, wide), BF),
        grid_spec=pltpu.PrefetchScalarGridSpec(
            num_scalar_prefetch=1,
            grid=(parts,),
            in_specs=specs,
            out_specs=pl.BlockSpec((1, rows, wide), lambda p, place: (p, 0, 0)),
        ),
        compiler_params=pltpu.CompilerParams(vmem_limit_bytes=48 << 20),
        cost_estimate=cost(18),
    )(jnp.zeros((2,), jnp.int32), *[array for term in terms for array in term])


def after(values, *earlier):
    return lax.optimization_barrier((values, *earlier))[0]


def wide_sum(*terms):
    total = terms[0].astype(F32)
    for term in terms[1:]:
        total = total + term.astype(F32)
    return total


def solution(mesh):
    dp, fsdp = mesh.shape["dp"], mesh.shape["fsdp"]
    assert fsdp == GROUP and dp % GROUP == 0
    inner = dp // GROUP

    def swap(values, r):
        return lax.ppermute(values, "fsdp", [(i, i ^ r) for i in range(fsdp)])

    def across(values):
        return lax.ppermute(values, "dp", [(i, i ^ 1) for i in range(dp)])

    def gather_blocks(values, chip=None):
        chip = swap(values, 2) if chip is None else chip
        return values, swap(values, 1), chip, swap(chip, 1)

    def gather_rows(values, chip=None):
        return jnp.concatenate(gather_blocks(values, chip), axis=0)

    def core_sum(terms):
        blocks = terms.reshape((GROUP, -1) + terms.shape[1:])
        got = swap(low(blocks[1::2]), 1)
        return wide_sum(blocks[0], got[0]), low(wide_sum(blocks[2], got[1]))

    def scatter_sum(terms):
        own, other = core_sum(terms)
        return own + swap(other, 2).astype(F32)

    def gather_plane(values, near=None):
        half = values.shape[0] // 2
        chip, side = near or (swap(values, 2), across(values))
        far = jnp.concatenate([across(chip[:half]), swap(side[half:], 2)], axis=0)
        blocks = [values, chip, side, far]
        mates = [swap(block, 1) for block in blocks]
        return jnp.concatenate([b for pair in zip(blocks, mates) for b in pair], axis=0)

    def plane_core(terms):
        blocks = terms.reshape((2 * GROUP, -1) + terms.shape[1:])
        got = swap(low(blocks[1::2]), 1)
        return [wide_sum(blocks[2 * i], got[i]) for i in range(GROUP)]

    def plane_far(sums):
        own, chip, side, far = sums
        half = far.shape[0] // 2
        top, bottom = across(low(far[:half])), swap(low(far[half:]), 2)
        chip = jnp.concatenate([wide_sum(chip[:half], top), chip[half:]], axis=0)
        side = jnp.concatenate([side[:half], wide_sum(side[half:], bottom)], axis=0)
        return own, low(chip), low(side)

    def plane_near(sums):
        own, chip, side = sums
        return own, swap(chip, 2), across(side)

    def pick(bit, low_part, high_part, axis):
        return jnp.where(
            bit == 0,
            jnp.concatenate([low_part, high_part], axis=axis),
            jnp.concatenate([high_part, low_part], axis=axis),
        )

    def sent_parts(weights, f, place, parts):
        rows, width = weights[0].shape[0], weights[0].shape[1] // GROUP
        size = rows // parts

        def part(weight, r):
            return lax.dynamic_slice(weight, (place * size, (f ^ r) * width), (size, width))

        return jnp.stack([jnp.stack([part(weight, 2), part(weight, 3)]) for weight in weights])

    def mate_parts(weights, f):
        rows, width = weights[0].shape[0], weights[0].shape[1] // GROUP
        sent = [lax.dynamic_slice(w, (0, (f ^ 1) * width), (rows, width)) for w in weights]
        return swap(jnp.stack(sent), 1)

    def head_pieces(weights, near, far, mate, mate_at=0):
        near_mate, far_mate = swap(near[:, 1], 1), swap(far[:, 1], 1)
        return [
            (
                weight,
                (mate, (i + mate_at,)),
                (near, (i, 0)),
                (far, (i, 0)),
                (near_mate, (i,)),
                (far_mate, (i,)),
            )
            for i, weight in enumerate(weights)
        ]

    def plain_sum(terms):
        parts = []
        for kind, left, right in terms:
            if kind == "owners":
                f = lax.axis_index("fsdp")
                size = left.shape[-2]
                right = right[0][:, :, right[1] * size : (right[1] + 1) * size]
                part = jnp.einsum("srt,stc->src", left, right, preferred_element_type=F32)
                part = jnp.take(part, f ^ jnp.arange(GROUP), axis=0)
                part = part.reshape(GROUP, size, inner, -1).transpose(0, 2, 1, 3)
                parts.append(low(part).reshape((dp, size, -1)))
            elif kind == "columns":
                tall = left.reshape(GROUP, -1, left.shape[1])
                wide = right.reshape(right.shape[0], inner, -1)
                part = jnp.einsum("zrt,txc->zxrc", tall, wide, preferred_element_type=F32)
                parts.append(low(part).reshape((dp,) + part.shape[2:]))
            else:
                wide = right.reshape(right.shape[0], dp, -1)
                parts.append(low(jnp.einsum("rt,tpc->prc", left, wide, preferred_element_type=F32)))
        grads = jnp.concatenate(parts, axis=1)
        return lax.psum_scatter(grads, "dp", scatter_dimension=0).astype(F32)

    def hop(values, bit):
        return lax.ppermute(values, "dp", [(i, i ^ (1 << bit)) for i in range(dp)])

    class Sum:
        def __init__(self, place, terms, order):
            self.place, self.terms, self.order = place, terms, order

        def send(self):
            if dp == 8:
                self.sent = half_grads(self.place, self.terms, self.order, 1)
            else:
                self.sent = self.total = plain_sum(self.terms)
            return self.sent

        def keep(self, *earlier):
            if dp == 8:
                first = after(self.terms[0][1], *earlier)
                terms = ((self.terms[0][0], first, self.terms[0][2]),) + self.terms[1:]
                self.kept = half_grads(self.place, terms, self.order, 0)
                return self.kept
            return self.sent

        def add(self, stage, *earlier):
            if dp != 8:
                return self.sent
            if stage == 1:
                self.one = after(hop(self.sent, self.order[0]), *earlier)
                self.sent = low(wide_sum(self.kept[2:], self.one[2:]))
                return self.sent
            if stage == 2:
                self.two = after(hop(self.sent, self.order[1]), *earlier)
                self.sent = low(wide_sum(self.kept[1], self.one[1], self.two[1]))
                return self.sent
            three = after(hop(self.sent, self.order[2]), *earlier)
            self.total = wide_sum(self.kept[0], self.one[0], self.two[0], three)
            return self.total

        def parts(self):
            out, at = [], 0
            for kind, left, right in self.terms:
                rows = left.shape[0] // GROUP if kind == "columns" else left.shape[-2]
                out.append(self.total[at : at + rows])
                at += rows
            return out

    def place_columns(values):
        pairs = []
        for z in range(GROUP):
            for x in range(inner):
                for f in range(GROUP):
                    pairs.append(((z * inner + x) * GROUP + f, (f * inner + x) * GROUP + z))
        return lax.ppermute(values, ("dp", "fsdp"), pairs)

    def on_device(
        tokens,
        patches,
        cotangent,
        lengths,
        episode_flags,
        norm_gains,
        w_query,
        w_key,
        w_value,
        w_out,
        c_query,
        c_key,
        c_value,
        c_out,
        patch_proj,
        w_gate,
        w_up,
        w_down,
    ):
        f = lax.axis_index("fsdp")
        x = lax.axis_index("dp") % 2
        z = (lax.axis_index("dp") // 2) % 2
        place = jnp.stack([f, lax.axis_index("dp")]).astype(jnp.int32)
        slot = tokens.shape[1]
        keys = patches.shape[1]
        width = tokens.shape[2] // GROUP
        inputs = tokens[0].astype(F32)
        bucket = jnp.where(
            lengths[0] <= slot // 4,
            slot // 4,
            jnp.where(lengths[0] <= slot // 2, slot // 2, slot),
        )
        live = (jnp.arange(slot, dtype=jnp.int32) < bucket).astype(F32)[:, None]
        grad_out = low(cotangent[0].astype(F32) * live)
        info = jnp.stack([lengths, episode_flags], axis=1)
        chip_info = swap(info, 2)
        w_query, w_key, w_value, inputs, chip_info = lax.optimization_barrier(
            (w_query, w_key, w_value, inputs, chip_info)
        )
        pair_near = swap(sent_parts((w_query, w_key), f, x, 2), 2)
        value_near = swap(sent_parts((w_value,), f, x, 2), 2)
        first = normed(inputs, norm_gains[0])
        first_chip = swap(first, 2)
        pair_far = across(pair_near)
        value_far = across(after(value_near, pair_far))

        rows = patch_proj.shape[0] // 4
        patch_in = after(patch_proj, pair_near, value_near)
        patch_mate = swap(patch_in, 1)
        patch_part = swap(lax.dynamic_slice_in_dim(patch_in, (2 * x + z) * rows, rows, 0), 2)
        patch_half = pick(z, patch_part, hop(patch_part, 1), 0)
        patch_chip = pick(x, patch_half, across(patch_half), 0)
        patch_far = swap(patch_chip, 1)
        cross_own = (c_key, c_value, c_query)
        cross_part = swap(sent_parts(after(cross_own, patch_part), f, 2 * x + z, 4), 2)
        cross_near = pick(z, cross_part, hop(cross_part, 1), 2)
        cross_far = across(cross_near)
        self_mate = mate_parts((w_query, w_key, w_value), f)
        first_blocks = gather_blocks(first, after(first_chip, pair_far))
        info = jnp.concatenate([info, swap(info, 1), chip_info, swap(chip_info, 1)], axis=0)
        query_w, key_w = head_pieces((w_query, w_key), pair_near, pair_far, self_mate)
        (value_w,) = head_pieces((w_value,), value_near, value_far, self_mate, 2)
        queries = to_heads(place, first_blocks, query_w)
        keys_all = to_heads(place, first_blocks, key_w)
        values_all = to_heads(place, first_blocks, value_w)
        mixed = attend(info, queries, keys_all, values_all, slot, slot, width, True)
        own, other = core_sum(low(nn(after(mixed, cross_near, patch_half), w_out)))
        cross_mate = mate_parts(after(cross_own, other), f)
        sent_out = other
        other = swap(other, 2)
        after_self = inputs + own + other.astype(F32)
        second = normed(after_self, norm_gains[1])
        second_chip = swap(second, 2)
        patch_blocks = (patch_proj, patch_mate, patch_chip, patch_far)
        patch_mat = join(place, after(patch_blocks, sent_out))
        context = low(nn(after(patches[0], second), patch_mat))
        context_chip = swap(context, 2)
        second_chip, cross_far = lax.optimization_barrier((second_chip, cross_far))
        second_blocks = gather_blocks(second, second_chip)
        cross_key_w, cross_value_w, cross_query_w = head_pieces(
            cross_own, cross_near, cross_far, cross_mate
        )
        cross_q = to_heads(place, second_blocks, cross_query_w)
        context_blocks = gather_blocks(context, after(context_chip, cross_q))
        cross_k = to_heads(place, context_blocks, cross_key_w)
        cross_v = to_heads(place, context_blocks, cross_value_w)
        grad_early = after(grad_out, context)
        cross_v, *grad_near = lax.optimization_barrier(
            (cross_v, swap(grad_early, 2), across(grad_early))
        )
        cross_mixed = attend(info, cross_q, cross_k, cross_v, slot, keys, width, False)
        own, other = core_sum(low(nn(cross_mixed, c_out)))
        grad_all = gather_plane(grad_out, after(tuple(grad_near), other))
        other = after(swap(other, 2), grad_all)
        after_cross = after_self + own + other.astype(F32)
        third = normed(after_cross, norm_gains[2])
        third_all = gather_plane(third)
        patch_width = patch_proj.shape[0]
        patch_rows = after(patches[0], third_all)

        def patch_piece(r):
            return lax.dynamic_slice(patch_rows, (0, (f ^ r) * patch_width), (keys, patch_width))

        patch_pieces = [patch_piece(0)] + [swap(patch_piece(r), r) for r in range(1, GROUP)]

        units = w_gate.shape[0] // 2
        gate_half, up_half, down_half = (
            lax.dynamic_slice_in_dim(w, x * units, units, 0) for w in (w_gate, w_up, w_down)
        )
        gate = nt(third_all, gate_half)
        up = nt(third_all, up_half)
        value, slope = gelu_parts(gate)
        hidden = low(value * up)
        grad_hidden = nt(grad_all, down_half)
        grad_gate = low(grad_hidden * up * slope)
        grad_up = low(grad_hidden * value)
        grad_gate, *patch_pieces = lax.optimization_barrier((grad_gate, *patch_pieces))
        third_part = low(nn(grad_gate, gate_half) + nn(grad_up, up_half))
        sums = plane_far(plane_core(third_part))
        hidden_terms = tuple(
            (turn(after(left, third_part)), right)
            for left, right in ((grad_gate, third_all), (grad_up, third_all), (hidden, grad_all))
        )
        first_left = after(hidden_terms[0][0], sums[1], sums[2])
        hidden_terms = ((first_left, third_all),) + hidden_terms[1:]
        hidden_bundle = all_grads(dp // 2, hidden_terms)
        hidden_grads = lax.psum_scatter(
            hidden_bundle,
            "dp",
            scatter_dimension=0,
            axis_index_groups=[list(range(i, dp, 2)) for i in range(2)],
        )
        own, chip, side = plane_near(sums)
        grad_third = wide_sum(own, after(chip, hidden_bundle), side)

        grad_norm, gain_third = norm_back(after_cross, norm_gains[2], grad_third)
        grad_after_cross = grad_out.astype(F32) + grad_norm
        grad_cross_out = low(grad_after_cross)
        cross_turned = turn(after(cross_mixed, grad_third))
        second_turned = turn(*after(second_blocks, grad_third))
        grad_cross_all = gather_rows(
            grad_cross_out, after(swap(grad_cross_out, 2), cross_turned, second_turned)
        )
        grad_cross_mixed = low(nt(grad_cross_all, c_out))
        grad_cq, grad_ck, grad_cv = attend_back(
            info, cross_q, cross_k, cross_v, grad_cross_mixed, slot, keys, width, False
        )
        own, other = core_sum(from_heads(place, (grad_cq,), (cross_query_w,)))
        context_turned = turn(*after(context_blocks, grad_cq))
        sum_cross = Sum(
            place,
            (("rows", cross_turned, grad_cross_all), ("columns", second_turned, grad_cq)),
            (0, 1, 2),
        )
        grad_second = own + after(swap(other, 2), sum_cross.send(), context_turned).astype(F32)

        grad_norm, gain_second = norm_back(after_self, norm_gains[1], grad_second)
        grad_after_self = grad_after_cross + grad_norm
        grad_self_out = low(grad_after_self)
        self_chip = swap(grad_self_out, 2)
        mixed_turned = turn(after(mixed, grad_self_out))
        first_turned = turn_own(place, after(first_blocks, grad_self_out), width)
        grad_self_all = gather_rows(
            grad_self_out,
            after(self_chip, mixed_turned, first_turned, sum_cross.keep(grad_self_out)),
        )
        grad_mixed = low(nt(grad_self_all, w_out))
        grad_q, grad_k, grad_v = attend_back(
            info, queries, keys_all, values_all, grad_mixed, slot, slot, width, True
        )
        heads = jnp.concatenate([grad_q, grad_k, grad_v], axis=1)
        heads_chip = swap(heads, 2)
        cross_one = sum_cross.add(1, grad_q)
        own, other = core_sum(
            from_heads(place, (after(grad_q, cross_one), grad_k, grad_v), (query_w, key_w, value_w))
        )
        other = swap(other, 2)
        sum_context = Sum(
            place,
            (
                ("columns", context_turned, grad_ck),
                ("columns", context_turned, grad_cv),
                ("rows", mixed_turned, grad_self_all),
            ),
            (0, 1, 2),
        )
        context_part = from_heads(
            place, (after(grad_ck, heads_chip), grad_cv), (cross_key_w, cross_value_w)
        )
        grad_first = own + after(
            other, sum_context.send(), context_part, hidden_grads, heads_chip
        ).astype(F32)
        grad_norm, gain_first = norm_back(inputs, norm_gains[0], grad_first)
        tokens_grad = (grad_after_self + grad_norm)[None]
        context_own, context_other = core_sum(context_part)
        context_other = swap(context_other, 2)
        gains = jnp.stack([gain_first, gain_second, gain_third])
        heads_all = jnp.stack([heads, swap(heads, 1), heads_chip, swap(heads_chip, 1)])
        sum_self = Sum(
            place,
            (("owners", first_turned, (heads_all, 0)), ("owners", first_turned, (heads_all, 1))),
            (0, 1, 2),
        )
        sum_value = Sum(place, (("owners", first_turned, (heads_all, 2)),), (1, 0, 2))
        kept = sum_context.keep(sum_self.send(), sum_value.send())
        step = sum_cross.add(2, kept)
        patch_turned = turn(*after(tuple(patch_pieces), kept))
        grad_context = low(context_own + after(context_other, kept, patch_turned).astype(F32))
        context_chip = swap(grad_context, 2)
        for bit in reversed(range(2, dp.bit_length() - 1)):
            gains = gains + after(hop(gains, bit), patch_turned)
        gains = gains + after(hop(gains, 1), grad_context)
        kept = sum_self.keep(grad_context, gains), sum_value.keep(grad_context)
        value_one = sum_value.add(1, *kept)
        cross_all = sum_cross.add(3, value_one)
        context_one = sum_context.add(1, cross_all)
        context_chip = after(context_chip, context_one)
        grad_context_all = gather_rows(grad_context, context_chip)
        sum_patch = Sum(place, (("rows", patch_turned, grad_context_all),), (1, 0, 2))
        sum_patch.send()
        step = sum_context.add(2, sum_patch.keep(sum_patch.sent))
        step = sum_self.add(1, step)
        out_part = low(nn(after(hidden, step), down_half))
        sums = plane_core(out_part)
        patches_grad = nt(after(grad_context, step), patch_mat)[None]
        own, chip, side = plane_far(after(tuple(sums), step))
        step = sum_patch.add(1, step, patches_grad, chip, side)
        columns = tokens.shape[2] // dp
        hidden_grads = after(hidden_grads, chip, side)
        hidden_other = across(
            lax.dynamic_slice_in_dim(hidden_grads, (1 - x) * columns, columns, 1)
        )
        step = sum_value.add(2, step)
        step = sum_self.add(2, step)
        own, chip, side = plane_near((own, chip, side))
        step = sum_patch.add(2, step)
        out_tokens = low((after_cross + wide_sum(own, after(chip, step), side)) * live)[None]
        gains = gains + after(hop(after(gains, step), 0), out_tokens)
        gains = gains + after(swap(gains, 2), out_tokens)
        gains_grad = gains + after(swap(gains, 1), out_tokens)
        step = sum_context.add(3, step, gains_grad)
        c_out_grad, c_query_grad = sum_cross.parts()
        c_key_grad, c_value_grad, w_out_grad = sum_context.parts()
        moved = place_columns(low(jnp.stack([c_query_grad, c_key_grad, c_value_grad])))
        hidden_mine = lax.dynamic_slice_in_dim(hidden_grads, x * columns, columns, 1)
        hidden_mine, hidden_other = after((hidden_mine, hidden_other), step)

        def both_halves(i):
            mine, other = (
                half[i * units : (i + 1) * units] for half in (hidden_mine, hidden_other)
            )
            return jnp.where(
                x == 0,
                jnp.concatenate([mine, other], axis=0),
                jnp.concatenate([other, mine], axis=0),
            ).astype(F32)

        gate_grad, up_grad, down_grad = (both_halves(i) for i in range(3))
        step = sum_value.add(3, step, gate_grad)
        step = sum_patch.add(3, step)
        step = sum_self.add(3, step)
        c_query_grad, c_key_grad, c_value_grad = after(moved, step).astype(F32)

        w_query_grad, w_key_grad = sum_self.parts()
        (w_value_grad,), (patch_proj_grad,) = sum_value.parts(), sum_patch.parts()

        return (
            out_tokens,
            tokens_grad,
            patches_grad,
            gains_grad,
            w_query_grad,
            w_key_grad,
            w_value_grad,
            w_out_grad,
            c_query_grad,
            c_key_grad,
            c_value_grad,
            c_out_grad,
            patch_proj_grad,
            gate_grad,
            up_grad,
            down_grad,
        )

    both, rows, block = ("dp", "fsdp"), P("fsdp", None), P("fsdp", "dp")
    whole = P(both, None, None)
    return jax.shard_map(
        on_device,
        mesh=mesh,
        in_specs=(whole, whole, whole, P(both), P(both), P()) + (rows,) * 12,
        out_specs=(whole, whole, whole, P()) + (block,) * 12,
        check_vma=False,
    )
```

```python
import functools

import jax
import jax.numpy as jnp
from jax import lax
from jax.experimental import pallas as pl
from jax.experimental.pallas import tpu as pltpu
from jax.sharding import PartitionSpec as P

HD = 128
SCALE = HD ** (-0.5)
EPS = 1e-06
BF = jnp.bfloat16
F32 = jnp.float32
GROUP = 4


def cost(us):
    return pl.CostEstimate(
        flops=int(us * 8e8), bytes_accessed=int(us * 2e6), transcendentals=0
    )


def low(v):
    return v.astype(BF)


def dot(left, right, left_dim, right_dim):
    return lax.dot_general(
        left, right, (((left_dim,), (right_dim,)), ((), ())), preferred_element_type=F32
    )


def nn(left, right):
    return dot(left, right, 1, 0)


def nt(left, right):
    return dot(left, right, 1, 1)


def tn(left, right):
    return dot(left, right, 0, 0)


def normed(values, gain):
    return low(values * lax.rsqrt(jnp.mean(values * values, axis=-1, keepdims=True) + EPS) * gain)


def norm_back(values, gain, grad):
    scale = lax.rsqrt(jnp.mean(values * values, axis=-1, keepdims=True) + EPS)
    unit = values * scale
    weighted = grad * gain
    grad_values = scale * (weighted - unit * jnp.mean(weighted * unit, axis=-1, keepdims=True))
    return grad_values, jnp.sum(grad * unit, axis=0)


def gelu_parts(v):
    c = 0.7978845608028654
    t = jnp.tanh(c * (v + 0.044715 * (v * v * v)))
    value = 0.5 * v * (1.0 + t)
    slope = 0.5 * (1.0 + t) + 0.5 * v * (1.0 - t * t) * (c * (1.0 + 3 * 0.044715 * v * v))
    return value, slope


def allowed_at(info, rows, columns):
    length = info[pl.program_id(0), 0]
    flag = info[pl.program_id(0), 1]
    prefix = jnp.where(flag == 0, length // 2, 0)
    query = lax.broadcasted_iota(jnp.int32, (rows, columns), 0)
    key = lax.broadcasted_iota(jnp.int32, (rows, columns), 1)
    return (key < length) & ((key <= query) | (key < prefix))


def probabilities(q, k, allowed):
    scores = nt(q, k) * SCALE
    if allowed is not None:
        scores = jnp.where(allowed, scores, -1e30)
    weights = jnp.exp(scores - jnp.max(scores, axis=-1, keepdims=True))
    return weights / jnp.sum(weights, axis=-1, keepdims=True)


def attend_kernel(masked, info, q_ref, k_ref, v_ref, out_ref):
    allowed = allowed_at(info, q_ref.shape[0], k_ref.shape[0]) if masked else None
    for head in range(q_ref.shape[1] // HD):
        at = pl.ds(head * HD, HD)
        probs = probabilities(q_ref[:, at], k_ref[:, at], allowed)
        out_ref[:, at] = low(nn(low(probs), v_ref[:, at]))


def attend_back_kernel(masked, info, q_ref, k_ref, v_ref, g_ref, gq_ref, gk_ref, gv_ref):
    allowed = allowed_at(info, q_ref.shape[0], k_ref.shape[0]) if masked else None
    for head in range(q_ref.shape[1] // HD):
        at = pl.ds(head * HD, HD)
        q, k, v, g = q_ref[:, at], k_ref[:, at], v_ref[:, at], g_ref[:, at]
        probs = probabilities(q, k, allowed)
        grad_probs = nt(g, v)
        gv_ref[:, at] = low(tn(low(probs), g))
        total = jnp.sum(probs * grad_probs, axis=-1, keepdims=True)
        grad_scores = low(probs * (grad_probs - total))
        gq_ref[:, at] = low(nn(grad_scores, k) * SCALE)
        gk_ref[:, at] = low(tn(grad_scores, q) * SCALE)


def head_block(rows, width):
    return pl.BlockSpec((rows, width), lambda s, info: (s, 0))


def attend(info, q, k, v, rows, keys, width, masked):
    return pl.pallas_call(
        functools.partial(attend_kernel, masked),
        out_shape=jax.ShapeDtypeStruct((GROUP * rows, width), BF),
        grid_spec=pltpu.PrefetchScalarGridSpec(
            num_scalar_prefetch=1,
            grid=(GROUP,),
            in_specs=[
                head_block(rows, width),
                head_block(keys, width),
                head_block(keys, width),
            ],
            out_specs=head_block(rows, width),
        ),
        compiler_params=pltpu.CompilerParams(vmem_limit_bytes=24 << 20),
        cost_estimate=cost(6 if masked else 4),
    )(info, q, k, v)


def attend_back(info, q, k, v, grad, rows, keys, width, masked):
    return pl.pallas_call(
        functools.partial(attend_back_kernel, masked),
        out_shape=(
            jax.ShapeDtypeStruct((GROUP * rows, width), BF),
            jax.ShapeDtypeStruct((GROUP * keys, width), BF),
            jax.ShapeDtypeStruct((GROUP * keys, width), BF),
        ),
        grid_spec=pltpu.PrefetchScalarGridSpec(
            num_scalar_prefetch=1,
            grid=(GROUP,),
            in_specs=[
                head_block(rows, width),
                head_block(keys, width),
                head_block(keys, width),
                head_block(rows, width),
            ],
            out_specs=(
                head_block(rows, width),
                head_block(keys, width),
                head_block(keys, width),
            ),
        ),
        compiler_params=pltpu.CompilerParams(vmem_limit_bytes=24 << 20),
        cost_estimate=cost(8),
    )(info, q, k, v, grad)


def placed(place, pieces):
    rows = pieces[0].shape[0]
    half = rows // 2
    f, x = place[0], place[1] % 2

    def at(block, part):
        return pl.multiple_of((f ^ block) * rows + part * half, half)

    spots = (
        pl.ds(at(0, 0), rows),
        pl.ds(at(1, 0), rows),
        pl.ds(at(2, x), half),
        pl.ds(at(2, 1 - x), half),
        pl.ds(at(3, x), half),
        pl.ds(at(3, 1 - x), half),
    )
    return tuple(zip(pieces, spots))


def row_tiles(rows, body):
    size = next((size for size in (512, 640) if rows % size == 0), rows)
    if size == rows:
        body(pl.ds(0, rows))
    else:
        pl.loop(0, rows // size)(lambda i: body(pl.ds(pl.multiple_of(i * size, size), size)))


def to_heads_kernel(count, place, *refs):
    pieces, out_ref = placed(place, refs[count : count + 6]), refs[count + 6]
    start = 0
    for rows_ref in refs[:count]:
        total = None
        for piece, features in pieces:
            term = nn(rows_ref[:, features], piece[...])
            total = term if total is None else total + term
        out_ref[pl.ds(start, rows_ref.shape[0]), :] = low(total)
        start += rows_ref.shape[0]


def from_heads_kernel(count, place, *refs):
    grads, pieces, out_ref = refs[:count], refs[count:-1], refs[-1]

    def tile(at):
        for part in range(6):
            total = None
            for i in range(count):
                piece, features = placed(place, pieces[6 * i : 6 * i + 6])[part]
                term = nt(grads[i][at, :], piece[...])
                total = term if total is None else total + term
            out_ref[at, features] = low(total)

    row_tiles(out_ref.shape[0], tile)


def piece_specs(pieces):
    rows, width = pieces[0].shape[0], pieces[1][0].shape[-1]
    specs = [pl.BlockSpec((rows, width), lambda i, place: (0, place[0]))]
    for array, at in pieces[1:]:
        block = (None,) * len(at) + array.shape[len(at) :]
        specs.append(pl.BlockSpec(block, lambda i, place, at=at: (*at, 0, 0)))
    return specs


def piece_arrays(pieces):
    return [pieces[0]] + [array for array, at in pieces[1:]]


def fixed(array):
    return pl.BlockSpec(array.shape, lambda i, place: (0, 0))


def to_heads(place, blocks, pieces):
    out = (sum(block.shape[0] for block in blocks), pieces[1][0].shape[-1])
    return pl.pallas_call(
        functools.partial(to_heads_kernel, len(blocks)),
        out_shape=jax.ShapeDtypeStruct(out, BF),
        grid_spec=pltpu.PrefetchScalarGridSpec(
            num_scalar_prefetch=1,
            grid=(1,),
            in_specs=[fixed(block) for block in blocks] + piece_specs(pieces),
            out_specs=pl.BlockSpec(out, lambda i, place: (0, 0)),
        ),
        compiler_params=pltpu.CompilerParams(vmem_limit_bytes=48 << 20),
        cost_estimate=cost(out[0] / 190),
    )(place, *blocks, *piece_arrays(pieces))


def from_heads(place, grads, weights):
    count = len(weights)
    out = (grads[0].shape[0], weights[0][0].shape[1])
    specs = [spec for pieces in weights for spec in piece_specs(pieces)]
    return pl.pallas_call(
        functools.partial(from_heads_kernel, count),
        out_shape=jax.ShapeDtypeStruct(out, BF),
        grid_spec=pltpu.PrefetchScalarGridSpec(
            num_scalar_prefetch=1,
            grid=(1,),
            in_specs=[fixed(g) for g in grads] + specs,
            out_specs=pl.BlockSpec(out, lambda i, place: (0, 0)),
        ),
        compiler_params=pltpu.CompilerParams(vmem_limit_bytes=56 << 20),
        cost_estimate=cost(3 + out[0] * count / 230),
    )(place, *grads, *[array for pieces in weights for array in piece_arrays(pieces)])


def half_kernel(place, *refs):
    lefts, rights, out_ref = refs[0:-1:2], refs[1:-1:2], refs[-1]
    start = 0
    for left, right in zip(lefts, rights):

        def product(at, start=start, left=left, right=right):
            out_ref[0, pl.ds(pl.multiple_of(start + at.start, 16), at.size), :] = low(
                nn(left[at, :], right[...])
            )

        row_tiles(left.shape[0], product)
        start += left.shape[0]


def half_grads(place, terms, order, side):
    def target(k, place):
        rel = (side << order[0]) + ((k // 2) << order[1]) + ((k % 2) << order[2])
        return place[1] ^ rel

    def source(k, place):
        return (target(k, place) // 2) ^ place[0]

    specs, arrays = [], []
    rows = 0
    for kind, left, right in terms:
        tall, tokens = left.shape[-2:]
        if kind == "columns":
            tall, wide = tall // GROUP, right.shape[1] // 2
            specs.append(pl.BlockSpec((tall, tokens), lambda k, place: (target(k, place) // 2, 0)))
            specs.append(pl.BlockSpec((tokens, wide), lambda k, place: (0, target(k, place) % 2)))
        elif kind == "owners":
            right, column = right
            wide = left.shape[-2] // 2
            specs.append(
                pl.BlockSpec((None, tall, tokens), lambda k, place: (source(k, place), 0, 0))
            )
            specs.append(
                pl.BlockSpec(
                    (None, tokens, wide),
                    lambda k, place, column=column: (
                        source(k, place),
                        0,
                        2 * column + target(k, place) % 2,
                    ),
                )
            )
        else:
            wide = right.shape[1] // 8
            specs.append(pl.BlockSpec((tall, tokens), lambda k, place: (0, 0)))
            specs.append(pl.BlockSpec((tokens, wide), lambda k, place: (0, target(k, place))))
        arrays += [left, right]
        rows += tall
    return pl.pallas_call(
        half_kernel,
        out_shape=jax.ShapeDtypeStruct((4, rows, wide), BF),
        grid_spec=pltpu.PrefetchScalarGridSpec(
            num_scalar_prefetch=1,
            grid=(4,),
            in_specs=specs,
            out_specs=pl.BlockSpec((1, rows, wide), lambda k, place: (k, 0, 0)),
        ),
        compiler_params=pltpu.CompilerParams(vmem_limit_bytes=48 << 20),
        cost_estimate=cost(rows / 210),
    )(place, *arrays)


def turn_kernel(*refs):
    start = 0
    for block in refs[:-1]:
        rows = block.shape[0]
        refs[-1][:, pl.ds(start, rows)] = block[...].T
        start += rows


def turn(*blocks):
    width = blocks[0].shape[1]
    step = 512 if width % 512 == 0 else width
    rows = sum(block.shape[0] for block in blocks)
    return pl.pallas_call(
        turn_kernel,
        out_shape=jax.ShapeDtypeStruct((width, rows), BF),
        grid=(width // step,),
        in_specs=[pl.BlockSpec((block.shape[0], step), lambda i: (0, i)) for block in blocks],
        out_specs=pl.BlockSpec((step, rows), lambda i: (i, 0)),
        compiler_params=pltpu.CompilerParams(vmem_limit_bytes=32 << 20),
        cost_estimate=cost(3),
    )(*blocks)


def turn_own_kernel(place, *refs):
    blocks, out_ref = refs[:-1], refs[-1]
    rows = blocks[0].shape[0]
    for k, block in enumerate(blocks):
        turned = block[...].T
        for r in range(GROUP):
            out_ref[r, :, pl.ds((k ^ r) * rows, rows)] = turned


def turn_own(place, blocks, width):
    rows = blocks[0].shape[0]
    out = (GROUP, width, GROUP * rows)
    return pl.pallas_call(
        turn_own_kernel,
        out_shape=jax.ShapeDtypeStruct(out, BF),
        grid_spec=pltpu.PrefetchScalarGridSpec(
            num_scalar_prefetch=1,
            grid=(1,),
            in_specs=[pl.BlockSpec((rows, width), lambda i, place: (0, place[0]))] * GROUP,
            out_specs=pl.BlockSpec(out, lambda i, place: (0, 0, 0)),
        ),
        compiler_params=pltpu.CompilerParams(vmem_limit_bytes=32 << 20),
        cost_estimate=cost(3),
    )(place, *blocks)


def join_kernel(place, *refs):
    for r, block in enumerate(refs[:-1]):

        @pl.when(pl.program_id(0) == r)
        def _():
            refs[-1][...] = block[...]


def join(place, blocks):
    rows, width = blocks[0].shape
    return pl.pallas_call(
        join_kernel,
        out_shape=jax.ShapeDtypeStruct((GROUP * rows, width), BF),
        grid_spec=pltpu.PrefetchScalarGridSpec(
            num_scalar_prefetch=1,
            grid=(GROUP,),
            in_specs=[fixed(block) for block in blocks],
            out_specs=pl.BlockSpec((rows, width), lambda i, place: (place[0] ^ i, 0)),
        ),
        compiler_params=pltpu.CompilerParams(vmem_limit_bytes=40 << 20),
        cost_estimate=cost(5),
    )(place, *blocks)


def all_grads(parts, terms):
    rows = sum(left.shape[0] for left, right in terms)
    wide = terms[0][1].shape[1] // parts
    specs = []
    for left, right in terms:
        specs.append(pl.BlockSpec(left.shape, lambda p, place: (0, 0)))
        specs.append(pl.BlockSpec((right.shape[0], wide), lambda p, place: (0, p)))
    return pl.pallas_call(
        half_kernel,
        out_shape=jax.ShapeDtypeStruct((parts, rows, wide), BF),
        grid_spec=pltpu.PrefetchScalarGridSpec(
            num_scalar_prefetch=1,
            grid=(parts,),
            in_specs=specs,
            out_specs=pl.BlockSpec((1, rows, wide), lambda p, place: (p, 0, 0)),
        ),
        compiler_params=pltpu.CompilerParams(vmem_limit_bytes=48 << 20),
        cost_estimate=cost(18),
    )(jnp.zeros((2,), jnp.int32), *[array for term in terms for array in term])


def after(values, *earlier):
    return lax.optimization_barrier((values, *earlier))[0]


def wide_sum(*terms):
    total = terms[0].astype(F32)
    for term in terms[1:]:
        total = total + term.astype(F32)
    return total


def solution(mesh):
    dp, fsdp = mesh.shape["dp"], mesh.shape["fsdp"]
    assert fsdp == GROUP and dp % GROUP == 0
    inner = dp // GROUP

    def swap(values, r):
        return lax.ppermute(values, "fsdp", [(i, i ^ r) for i in range(fsdp)])

    def across(values):
        return lax.ppermute(values, "dp", [(i, i ^ 1) for i in range(dp)])

    def gather_blocks(values, chip=None):
        chip = swap(values, 2) if chip is None else chip
        return values, swap(values, 1), chip, swap(chip, 1)

    def gather_rows(values, chip=None):
        return jnp.concatenate(gather_blocks(values, chip), axis=0)

    def core_sum(terms):
        blocks = terms.reshape((GROUP, -1) + terms.shape[1:])
        got = swap(low(blocks[1::2]), 1)
        return wide_sum(blocks[0], got[0]), low(wide_sum(blocks[2], got[1]))

    def scatter_sum(terms):
        own, other = core_sum(terms)
        return own + swap(other, 2).astype(F32)

    def gather_plane(values, near=None):
        half = values.shape[0] // 2
        chip, side = near or (swap(values, 2), across(values))
        far = jnp.concatenate([across(chip[:half]), swap(side[half:], 2)], axis=0)
        blocks = [values, chip, side, far]
        mates = [swap(block, 1) for block in blocks]
        return jnp.concatenate([b for pair in zip(blocks, mates) for b in pair], axis=0)

    def plane_core(terms):
        blocks = terms.reshape((2 * GROUP, -1) + terms.shape[1:])
        got = swap(low(blocks[1::2]), 1)
        return [wide_sum(blocks[2 * i], got[i]) for i in range(GROUP)]

    def plane_far(sums):
        own, chip, side, far = sums
        half = far.shape[0] // 2
        top, bottom = across(low(far[:half])), swap(low(far[half:]), 2)
        chip = jnp.concatenate([wide_sum(chip[:half], top), chip[half:]], axis=0)
        side = jnp.concatenate([side[:half], wide_sum(side[half:], bottom)], axis=0)
        return own, low(chip), low(side)

    def plane_near(sums):
        own, chip, side = sums
        return own, swap(chip, 2), across(side)

    def pick(bit, low_part, high_part, axis):
        return jnp.where(
            bit == 0,
            jnp.concatenate([low_part, high_part], axis=axis),
            jnp.concatenate([high_part, low_part], axis=axis),
        )

    def sent_parts(weights, f, place, parts):
        rows, width = weights[0].shape[0], weights[0].shape[1] // GROUP
        size = rows // parts

        def part(weight, r):
            return lax.dynamic_slice(weight, (place * size, (f ^ r) * width), (size, width))

        return jnp.stack([jnp.stack([part(weight, 2), part(weight, 3)]) for weight in weights])

    def mate_parts(weights, f):
        rows, width = weights[0].shape[0], weights[0].shape[1] // GROUP
        sent = [lax.dynamic_slice(w, (0, (f ^ 1) * width), (rows, width)) for w in weights]
        return swap(jnp.stack(sent), 1)

    def head_pieces(weights, near, far, mate, mate_at=0):
        near_mate, far_mate = swap(near[:, 1], 1), swap(far[:, 1], 1)
        return [
            (
                weight,
                (mate, (i + mate_at,)),
                (near, (i, 0)),
                (far, (i, 0)),
                (near_mate, (i,)),
                (far_mate, (i,)),
            )
            for i, weight in enumerate(weights)
        ]

    def plain_sum(terms):
        parts = []
        for kind, left, right in terms:
            if kind == "owners":
                f = lax.axis_index("fsdp")
                size = left.shape[-2]
                right = right[0][:, :, right[1] * size : (right[1] + 1) * size]
                part = jnp.einsum("srt,stc->src", left, right, preferred_element_type=F32)
                part = jnp.take(part, f ^ jnp.arange(GROUP), axis=0)
                part = part.reshape(GROUP, size, inner, -1).transpose(0, 2, 1, 3)
                parts.append(low(part).reshape((dp, size, -1)))
            elif kind == "columns":
                tall = left.reshape(GROUP, -1, left.shape[1])
                wide = right.reshape(right.shape[0], inner, -1)
                part = jnp.einsum("zrt,txc->zxrc", tall, wide, preferred_element_type=F32)
                parts.append(low(part).reshape((dp,) + part.shape[2:]))
            else:
                wide = right.reshape(right.shape[0], dp, -1)
                parts.append(low(jnp.einsum("rt,tpc->prc", left, wide, preferred_element_type=F32)))
        grads = jnp.concatenate(parts, axis=1)
        return lax.psum_scatter(grads, "dp", scatter_dimension=0).astype(F32)

    def hop(values, bit):
        return lax.ppermute(values, "dp", [(i, i ^ (1 << bit)) for i in range(dp)])

    class Sum:
        def __init__(self, place, terms, order):
            self.place, self.terms, self.order = place, terms, order

        def send(self):
            if dp == 8:
                self.sent = half_grads(self.place, self.terms, self.order, 1)
            else:
                self.sent = self.total = plain_sum(self.terms)
            return self.sent

        def keep(self, *earlier):
            if dp == 8:
                first = after(self.terms[0][1], *earlier)
                terms = ((self.terms[0][0], first, self.terms[0][2]),) + self.terms[1:]
                self.kept = half_grads(self.place, terms, self.order, 0)
                return self.kept
            return self.sent

        def add(self, stage, *earlier):
            if dp != 8:
                return self.sent
            if stage == 1:
                self.one = after(hop(self.sent, self.order[0]), *earlier)
                self.sent = low(wide_sum(self.kept[2:], self.one[2:]))
                return self.sent
            if stage == 2:
                self.two = after(hop(self.sent, self.order[1]), *earlier)
                self.sent = low(wide_sum(self.kept[1], self.one[1], self.two[1]))
                return self.sent
            three = after(hop(self.sent, self.order[2]), *earlier)
            self.total = wide_sum(self.kept[0], self.one[0], self.two[0], three)
            return self.total

        def parts(self):
            out, at = [], 0
            for kind, left, right in self.terms:
                rows = left.shape[0] // GROUP if kind == "columns" else left.shape[-2]
                out.append(self.total[at : at + rows])
                at += rows
            return out

    def place_columns(values):
        pairs = []
        for z in range(GROUP):
            for x in range(inner):
                for f in range(GROUP):
                    pairs.append(((z * inner + x) * GROUP + f, (f * inner + x) * GROUP + z))
        return lax.ppermute(values, ("dp", "fsdp"), pairs)

    def on_device(
        tokens,
        patches,
        cotangent,
        lengths,
        episode_flags,
        norm_gains,
        w_query,
        w_key,
        w_value,
        w_out,
        c_query,
        c_key,
        c_value,
        c_out,
        patch_proj,
        w_gate,
        w_up,
        w_down,
    ):
        f = lax.axis_index("fsdp")
        x = lax.axis_index("dp") % 2
        z = (lax.axis_index("dp") // 2) % 2
        place = jnp.stack([f, lax.axis_index("dp")]).astype(jnp.int32)
        slot = tokens.shape[1]
        keys = patches.shape[1]
        width = tokens.shape[2] // GROUP
        inputs = tokens[0].astype(F32)
        bucket = jnp.where(
            lengths[0] <= slot // 4,
            slot // 4,
            jnp.where(lengths[0] <= slot // 2, slot // 2, slot),
        )
        live = (jnp.arange(slot, dtype=jnp.int32) < bucket).astype(F32)[:, None]
        grad_out = low(cotangent[0].astype(F32) * live)
        info = jnp.stack([lengths, episode_flags], axis=1)
        chip_info = swap(info, 2)
        w_query, w_key, w_value, inputs, chip_info = lax.optimization_barrier(
            (w_query, w_key, w_value, inputs, chip_info)
        )
        pair_near = swap(sent_parts((w_query, w_key), f, x, 2), 2)
        value_near = swap(sent_parts((w_value,), f, x, 2), 2)
        first = normed(inputs, norm_gains[0])
        first_chip = swap(first, 2)
        pair_far = across(pair_near)
        value_far = across(after(value_near, pair_far))

        rows = patch_proj.shape[0] // 4
        patch_in = after(patch_proj, pair_near)
        patch_mate = swap(patch_in, 1)
        patch_part = swap(lax.dynamic_slice_in_dim(patch_in, (2 * x + z) * rows, rows, 0), 2)
        patch_half = pick(z, patch_part, hop(patch_part, 1), 0)
        patch_chip = pick(x, patch_half, across(patch_half), 0)
        patch_far = swap(patch_chip, 1)
        cross_own = (c_key, c_value, c_query)
        cross_ready = after(cross_own, patch_part, value_near)
        cross_part = swap(sent_parts(cross_ready, f, 2 * x + z, 4), 2)
        cross_near = pick(z, cross_part, hop(cross_part, 1), 2)
        cross_far = across(cross_near)
        self_mate = mate_parts((w_query, w_key, w_value), f)
        first_blocks = gather_blocks(first, after(first_chip, pair_far))
        info = jnp.concatenate([info, swap(info, 1), chip_info, swap(chip_info, 1)], axis=0)
        query_w, key_w = head_pieces((w_query, w_key), pair_near, pair_far, self_mate)
        (value_w,) = head_pieces((w_value,), value_near, value_far, self_mate, 2)
        queries = to_heads(place, first_blocks, query_w)
        keys_all = to_heads(place, first_blocks, key_w)
        values_all = to_heads(place, first_blocks, value_w)
        mixed = attend(info, queries, keys_all, values_all, slot, slot, width, True)
        own, other = core_sum(low(nn(after(mixed, cross_near, patch_half), w_out)))
        cross_mate = mate_parts(after(cross_own, other), f)
        sent_out = other
        other = swap(other, 2)
        after_self = inputs + own + other.astype(F32)
        second = normed(after_self, norm_gains[1])
        second_chip = swap(second, 2)
        patch_blocks = (patch_proj, patch_mate, patch_chip, patch_far)
        patch_mat = join(place, after(patch_blocks, sent_out))
        context = low(nn(after(patches[0], second), patch_mat))
        context_chip = swap(context, 2)
        second_chip, cross_far = lax.optimization_barrier((second_chip, cross_far))
        second_blocks = gather_blocks(second, second_chip)
        cross_key_w, cross_value_w, cross_query_w = head_pieces(
            cross_own, cross_near, cross_far, cross_mate
        )
        cross_q = to_heads(place, second_blocks, cross_query_w)
        context_blocks = gather_blocks(context, after(context_chip, cross_q))
        cross_k = to_heads(place, context_blocks, cross_key_w)
        cross_v = to_heads(place, context_blocks, cross_value_w)
        cross_mixed = attend(info, cross_q, cross_k, cross_v, slot, keys, width, False)
        grad_early = after(grad_out, context)
        cross_mixed, *grad_near = lax.optimization_barrier(
            (cross_mixed, swap(grad_early, 2), across(grad_early))
        )
        own, other = core_sum(low(nn(cross_mixed, c_out)))
        grad_all = gather_plane(grad_out, tuple(grad_near))
        other = after(swap(other, 2), grad_all)
        after_cross = after_self + own + other.astype(F32)
        third = normed(after_cross, norm_gains[2])
        third_all = gather_plane(third)
        patch_width = patch_proj.shape[0]
        patch_rows = after(patches[0], third_all)

        def patch_piece(r):
            return lax.dynamic_slice(patch_rows, (0, (f ^ r) * patch_width), (keys, patch_width))

        patch_pieces = [patch_piece(0)] + [swap(patch_piece(r), r) for r in range(1, GROUP)]

        units = w_gate.shape[0] // 2
        gate_half, up_half, down_half = (
            lax.dynamic_slice_in_dim(w, x * units, units, 0) for w in (w_gate, w_up, w_down)
        )
        gate = nt(third_all, gate_half)
        up = nt(third_all, up_half)
        value, slope = gelu_parts(gate)
        hidden = low(value * up)
        grad_hidden = nt(grad_all, down_half)
        grad_gate = low(grad_hidden * up * slope)
        grad_up = low(grad_hidden * value)
        grad_gate, *patch_pieces = lax.optimization_barrier((grad_gate, *patch_pieces))
        third_part = low(nn(grad_gate, gate_half) + nn(grad_up, up_half))
        sums = plane_far(plane_core(third_part))
        hidden_terms = tuple(
            (turn(after(left, third_part)), right)
            for left, right in ((grad_gate, third_all), (grad_up, third_all), (hidden, grad_all))
        )
        first_left = after(hidden_terms[0][0], sums[1], sums[2])
        hidden_terms = ((first_left, third_all),) + hidden_terms[1:]
        hidden_bundle = all_grads(dp // 2, hidden_terms)
        hidden_grads = lax.psum_scatter(
            hidden_bundle,
            "dp",
            scatter_dimension=0,
            axis_index_groups=[list(range(i, dp, 2)) for i in range(2)],
        )
        own, chip, side = plane_near(sums)
        grad_third = wide_sum(own, after(chip, hidden_bundle), side)

        grad_norm, gain_third = norm_back(after_cross, norm_gains[2], grad_third)
        grad_after_cross = grad_out.astype(F32) + grad_norm
        grad_cross_out = low(grad_after_cross)
        cross_turned = turn(after(cross_mixed, grad_third))
        second_turned = turn(*after(second_blocks, grad_third))
        grad_cross_all = gather_rows(
            grad_cross_out, after(swap(grad_cross_out, 2), cross_turned, second_turned)
        )
        grad_cross_mixed = low(nt(grad_cross_all, c_out))
        grad_cq, grad_ck, grad_cv = attend_back(
            info, cross_q, cross_k, cross_v, grad_cross_mixed, slot, keys, width, False
        )
        own, other = core_sum(from_heads(place, (grad_cq,), (cross_query_w,)))
        context_turned = turn(*after(context_blocks, grad_cq))
        sum_cross = Sum(
            place,
            (("rows", cross_turned, grad_cross_all), ("columns", second_turned, grad_cq)),
            (0, 1, 2),
        )
        grad_second = own + after(swap(other, 2), sum_cross.send(), context_turned).astype(F32)

        grad_norm, gain_second = norm_back(after_self, norm_gains[1], grad_second)
        grad_after_self = grad_after_cross + grad_norm
        grad_self_out = low(grad_after_self)
        self_chip = swap(grad_self_out, 2)
        mixed_turned = turn(after(mixed, grad_self_out))
        first_turned = turn_own(place, after(first_blocks, grad_self_out), width)
        grad_self_all = gather_rows(
            grad_self_out,
            after(self_chip, mixed_turned, first_turned, sum_cross.keep(grad_self_out)),
        )
        grad_mixed = low(nt(grad_self_all, w_out))
        grad_q, grad_k, grad_v = attend_back(
            info, queries, keys_all, values_all, grad_mixed, slot, slot, width, True
        )
        heads = jnp.concatenate([grad_q, grad_k, grad_v], axis=1)
        heads_chip = swap(heads, 2)
        self_part = from_heads(place, (grad_q, grad_k, grad_v), (query_w, key_w, value_w))
        own, other = core_sum(self_part)
        other = swap(other, 2)
        cross_one = sum_cross.add(1, self_part)
        sum_context = Sum(
            place,
            (
                ("columns", context_turned, grad_ck),
                ("columns", context_turned, grad_cv),
                ("rows", mixed_turned, grad_self_all),
            ),
            (0, 1, 2),
        )
        context_part = from_heads(
            place, (after(grad_ck, heads_chip), grad_cv), (cross_key_w, cross_value_w)
        )
        grad_first = own + after(
            other, sum_context.send(), context_part, hidden_grads, heads_chip
        ).astype(F32)
        grad_norm, gain_first = norm_back(inputs, norm_gains[0], grad_first)
        tokens_grad = (grad_after_self + grad_norm)[None]
        context_own, context_other = core_sum(context_part)
        context_other = swap(context_other, 2)
        gains = jnp.stack([gain_first, gain_second, gain_third])
        heads_all = jnp.stack([heads, swap(heads, 1), heads_chip, swap(heads_chip, 1)])
        sum_self = Sum(
            place,
            (("owners", first_turned, (heads_all, 0)), ("owners", first_turned, (heads_all, 1))),
            (0, 1, 2),
        )
        sum_value = Sum(place, (("owners", first_turned, (heads_all, 2)),), (1, 0, 2))
        kept = sum_context.keep(sum_self.send(), sum_value.send())
        step = sum_cross.add(2, kept)
        patch_turned = turn(*after(tuple(patch_pieces), kept))
        grad_context = low(context_own + after(context_other, kept, patch_turned).astype(F32))
        context_chip = swap(grad_context, 2)
        for bit in reversed(range(2, dp.bit_length() - 1)):
            gains = gains + after(hop(gains, bit), patch_turned)
        gains = gains + after(hop(gains, 1), grad_context)
        kept = sum_self.keep(grad_context, gains), sum_value.keep(grad_context)
        value_one = sum_value.add(1, *kept)
        cross_all = sum_cross.add(3, value_one)
        context_one = sum_context.add(1, cross_all)
        context_chip = after(context_chip, context_one)
        grad_context_all = gather_rows(grad_context, context_chip)
        sum_patch = Sum(place, (("rows", patch_turned, grad_context_all),), (1, 0, 2))
        sum_patch.send()
        kept = sum_patch.keep(sum_patch.sent)
        out_part = low(nn(after(hidden, kept), down_half))
        sums = plane_core(out_part)
        patches_grad = nt(after(grad_context, kept), patch_mat)[None]
        step = sum_context.add(2, kept, out_part, patches_grad)
        step = sum_self.add(1, step)
        own, chip, side = plane_far(after(tuple(sums), step))
        step = sum_patch.add(1, step)
        step = sum_value.add(2, step)
        gains = gains + after(hop(after(gains, step), 0), chip, side)
        gains = gains + after(swap(gains, 2), chip)
        gains_grad = gains + after(swap(gains, 1), chip)
        step = sum_patch.add(2, step, chip, side, gains_grad)
        step = sum_self.add(2, step)
        columns = tokens.shape[2] // dp
        hidden_grads = after(hidden_grads, step)
        hidden_other = across(
            lax.dynamic_slice_in_dim(hidden_grads, (1 - x) * columns, columns, 1)
        )
        own, chip, side = plane_near((own, chip, side))
        step = sum_context.add(3, step)
        c_out_grad, c_query_grad = sum_cross.parts()
        c_key_grad, c_value_grad, w_out_grad = sum_context.parts()
        moved = place_columns(low(jnp.stack([c_query_grad, c_key_grad, c_value_grad])))
        step = sum_value.add(3, step, hidden_other)
        step = sum_self.add(3, step)
        out_tokens = low((after_cross + wide_sum(own, after(chip, step), side)) * live)[None]
        hidden_mine = lax.dynamic_slice_in_dim(hidden_grads, x * columns, columns, 1)
        hidden_mine, hidden_other = after((hidden_mine, hidden_other), step)

        def both_halves(i):
            mine, other = (
                half[i * units : (i + 1) * units] for half in (hidden_mine, hidden_other)
            )
            return jnp.where(
                x == 0,
                jnp.concatenate([mine, other], axis=0),
                jnp.concatenate([other, mine], axis=0),
            ).astype(F32)

        gate_grad, up_grad, down_grad = (both_halves(i) for i in range(3))
        step = sum_patch.add(3, step, gate_grad)
        c_query_grad, c_key_grad, c_value_grad = after(moved, step).astype(F32)

        w_query_grad, w_key_grad = sum_self.parts()
        (w_value_grad,), (patch_proj_grad,) = sum_value.parts(), sum_patch.parts()

        return (
            out_tokens,
            tokens_grad,
            patches_grad,
            gains_grad,
            w_query_grad,
            w_key_grad,
            w_value_grad,
            w_out_grad,
            c_query_grad,
            c_key_grad,
            c_value_grad,
            c_out_grad,
            patch_proj_grad,
            gate_grad,
            up_grad,
            down_grad,
        )

    both, rows, block = ("dp", "fsdp"), P("fsdp", None), P("fsdp", "dp")
    whole = P(both, None, None)
    return jax.shard_map(
        on_device,
        mesh=mesh,
        in_specs=(whole, whole, whole, P(both), P(both), P()) + (rows,) * 12,
        out_specs=(whole, whole, whole, P()) + (block,) * 12,
        check_vma=False,
    )
```

```python
import functools

import jax
import jax.numpy as jnp
from jax import lax
from jax.experimental import pallas as pl
from jax.experimental.pallas import tpu as pltpu
from jax.sharding import PartitionSpec as P

HD = 128
SCALE = HD ** (-0.5)
EPS = 1e-06
BF = jnp.bfloat16
F32 = jnp.float32
GROUP = 4


def cost(us):
    return pl.CostEstimate(
        flops=int(us * 8e8), bytes_accessed=int(us * 2e6), transcendentals=0
    )


def low(v):
    return v.astype(BF)


def dot(left, right, left_dim, right_dim):
    return lax.dot_general(
        left, right, (((left_dim,), (right_dim,)), ((), ())), preferred_element_type=F32
    )


def nn(left, right):
    return dot(left, right, 1, 0)


def nt(left, right):
    return dot(left, right, 1, 1)


def tn(left, right):
    return dot(left, right, 0, 0)


def normed(values, gain):
    return low(values * lax.rsqrt(jnp.mean(values * values, axis=-1, keepdims=True) + EPS) * gain)


def norm_back(values, gain, grad):
    scale = lax.rsqrt(jnp.mean(values * values, axis=-1, keepdims=True) + EPS)
    unit = values * scale
    weighted = grad * gain
    grad_values = scale * (weighted - unit * jnp.mean(weighted * unit, axis=-1, keepdims=True))
    return grad_values, jnp.sum(grad * unit, axis=0)


def gelu_parts(v):
    c = 0.7978845608028654
    t = jnp.tanh(c * (v + 0.044715 * (v * v * v)))
    value = 0.5 * v * (1.0 + t)
    slope = 0.5 * (1.0 + t) + 0.5 * v * (1.0 - t * t) * (c * (1.0 + 3 * 0.044715 * v * v))
    return value, slope


def allowed_at(info, rows, columns):
    length = info[pl.program_id(0), 0]
    flag = info[pl.program_id(0), 1]
    prefix = jnp.where(flag == 0, length // 2, 0)
    query = lax.broadcasted_iota(jnp.int32, (rows, columns), 0)
    key = lax.broadcasted_iota(jnp.int32, (rows, columns), 1)
    return (key < length) & ((key <= query) | (key < prefix))


def probabilities(q, k, allowed):
    scores = nt(q, k) * SCALE
    if allowed is not None:
        scores = jnp.where(allowed, scores, -1e30)
    weights = jnp.exp(scores - jnp.max(scores, axis=-1, keepdims=True))
    return weights / jnp.sum(weights, axis=-1, keepdims=True)


def attend_kernel(masked, info, q_ref, k_ref, v_ref, out_ref):
    allowed = allowed_at(info, q_ref.shape[0], k_ref.shape[0]) if masked else None
    for head in range(q_ref.shape[1] // HD):
        at = pl.ds(head * HD, HD)
        probs = probabilities(q_ref[:, at], k_ref[:, at], allowed)
        out_ref[:, at] = low(nn(low(probs), v_ref[:, at]))


def attend_back_kernel(masked, info, q_ref, k_ref, v_ref, g_ref, gq_ref, gk_ref, gv_ref):
    allowed = allowed_at(info, q_ref.shape[0], k_ref.shape[0]) if masked else None
    for head in range(q_ref.shape[1] // HD):
        at = pl.ds(head * HD, HD)
        q, k, v, g = q_ref[:, at], k_ref[:, at], v_ref[:, at], g_ref[:, at]
        probs = probabilities(q, k, allowed)
        grad_probs = nt(g, v)
        gv_ref[:, at] = low(tn(low(probs), g))
        total = jnp.sum(probs * grad_probs, axis=-1, keepdims=True)
        grad_scores = low(probs * (grad_probs - total))
        gq_ref[:, at] = low(nn(grad_scores, k) * SCALE)
        gk_ref[:, at] = low(tn(grad_scores, q) * SCALE)


def head_block(rows, width):
    return pl.BlockSpec((rows, width), lambda s, info: (s, 0))


def attend(info, q, k, v, rows, keys, width, masked):
    return pl.pallas_call(
        functools.partial(attend_kernel, masked),
        out_shape=jax.ShapeDtypeStruct((GROUP * rows, width), BF),
        grid_spec=pltpu.PrefetchScalarGridSpec(
            num_scalar_prefetch=1,
            grid=(GROUP,),
            in_specs=[
                head_block(rows, width),
                head_block(keys, width),
                head_block(keys, width),
            ],
            out_specs=head_block(rows, width),
        ),
        compiler_params=pltpu.CompilerParams(vmem_limit_bytes=24 << 20),
        cost_estimate=cost(6 if masked else 4),
    )(info, q, k, v)


def attend_back(info, q, k, v, grad, rows, keys, width, masked):
    return pl.pallas_call(
        functools.partial(attend_back_kernel, masked),
        out_shape=(
            jax.ShapeDtypeStruct((GROUP * rows, width), BF),
            jax.ShapeDtypeStruct((GROUP * keys, width), BF),
            jax.ShapeDtypeStruct((GROUP * keys, width), BF),
        ),
        grid_spec=pltpu.PrefetchScalarGridSpec(
            num_scalar_prefetch=1,
            grid=(GROUP,),
            in_specs=[
                head_block(rows, width),
                head_block(keys, width),
                head_block(keys, width),
                head_block(rows, width),
            ],
            out_specs=(
                head_block(rows, width),
                head_block(keys, width),
                head_block(keys, width),
            ),
        ),
        compiler_params=pltpu.CompilerParams(vmem_limit_bytes=24 << 20),
        cost_estimate=cost(8),
    )(info, q, k, v, grad)


def placed(place, pieces):
    rows = pieces[0].shape[0]
    half = rows // 2
    f, x = place[0], place[1] % 2

    def at(block, part):
        return pl.multiple_of((f ^ block) * rows + part * half, half)

    spots = (
        pl.ds(at(0, 0), rows),
        pl.ds(at(1, 0), rows),
        pl.ds(at(2, x), half),
        pl.ds(at(2, 1 - x), half),
        pl.ds(at(3, x), half),
        pl.ds(at(3, 1 - x), half),
    )
    return tuple(zip(pieces, spots))


def row_tiles(rows, body):
    size = next((size for size in (512, 640) if rows % size == 0), rows)
    if size == rows:
        body(pl.ds(0, rows))
    else:
        pl.loop(0, rows // size)(lambda i: body(pl.ds(pl.multiple_of(i * size, size), size)))


def to_heads_kernel(count, place, *refs):
    pieces, out_ref = placed(place, refs[count : count + 6]), refs[count + 6]
    start = 0
    for rows_ref in refs[:count]:
        total = None
        for piece, features in pieces:
            term = nn(rows_ref[:, features], piece[...])
            total = term if total is None else total + term
        out_ref[pl.ds(start, rows_ref.shape[0]), :] = low(total)
        start += rows_ref.shape[0]


def from_heads_kernel(count, place, *refs):
    grads, pieces, out_ref = refs[:count], refs[count:-1], refs[-1]

    def tile(at):
        for part in range(6):
            total = None
            for i in range(count):
                piece, features = placed(place, pieces[6 * i : 6 * i + 6])[part]
                term = nt(grads[i][at, :], piece[...])
                total = term if total is None else total + term
            out_ref[at, features] = low(total)

    row_tiles(out_ref.shape[0], tile)


def piece_specs(pieces):
    rows, width = pieces[0].shape[0], pieces[1][0].shape[-1]
    specs = [pl.BlockSpec((rows, width), lambda i, place: (0, place[0]))]
    for array, at in pieces[1:]:
        block = (None,) * len(at) + array.shape[len(at) :]
        specs.append(pl.BlockSpec(block, lambda i, place, at=at: (*at, 0, 0)))
    return specs


def piece_arrays(pieces):
    return [pieces[0]] + [array for array, at in pieces[1:]]


def fixed(array):
    return pl.BlockSpec(array.shape, lambda i, place: (0, 0))


def to_heads(place, blocks, pieces):
    out = (sum(block.shape[0] for block in blocks), pieces[1][0].shape[-1])
    return pl.pallas_call(
        functools.partial(to_heads_kernel, len(blocks)),
        out_shape=jax.ShapeDtypeStruct(out, BF),
        grid_spec=pltpu.PrefetchScalarGridSpec(
            num_scalar_prefetch=1,
            grid=(1,),
            in_specs=[fixed(block) for block in blocks] + piece_specs(pieces),
            out_specs=pl.BlockSpec(out, lambda i, place: (0, 0)),
        ),
        compiler_params=pltpu.CompilerParams(vmem_limit_bytes=48 << 20),
        cost_estimate=cost(out[0] / 190),
    )(place, *blocks, *piece_arrays(pieces))


def from_heads(place, grads, weights):
    count = len(weights)
    out = (grads[0].shape[0], weights[0][0].shape[1])
    specs = [spec for pieces in weights for spec in piece_specs(pieces)]
    return pl.pallas_call(
        functools.partial(from_heads_kernel, count),
        out_shape=jax.ShapeDtypeStruct(out, BF),
        grid_spec=pltpu.PrefetchScalarGridSpec(
            num_scalar_prefetch=1,
            grid=(1,),
            in_specs=[fixed(g) for g in grads] + specs,
            out_specs=pl.BlockSpec(out, lambda i, place: (0, 0)),
        ),
        compiler_params=pltpu.CompilerParams(vmem_limit_bytes=56 << 20),
        cost_estimate=cost(3 + out[0] * count / 230),
    )(place, *grads, *[array for pieces in weights for array in piece_arrays(pieces)])


def half_kernel(place, *refs):
    lefts, rights, out_ref = refs[0:-1:2], refs[1:-1:2], refs[-1]
    start = 0
    for left, right in zip(lefts, rights):

        def product(at, start=start, left=left, right=right):
            out_ref[0, pl.ds(pl.multiple_of(start + at.start, 16), at.size), :] = low(
                nn(left[at, :], right[...])
            )

        row_tiles(left.shape[0], product)
        start += left.shape[0]


def half_grads(place, terms, order, side):
    def target(k, place):
        rel = (side << order[0]) + ((k // 2) << order[1]) + ((k % 2) << order[2])
        return place[1] ^ rel

    def source(k, place):
        return (target(k, place) // 2) ^ place[0]

    specs, arrays = [], []
    rows = 0
    for kind, left, right in terms:
        tall, tokens = left.shape[-2:]
        if kind == "columns":
            tall, wide = tall // GROUP, right.shape[1] // 2
            specs.append(pl.BlockSpec((tall, tokens), lambda k, place: (target(k, place) // 2, 0)))
            specs.append(pl.BlockSpec((tokens, wide), lambda k, place: (0, target(k, place) % 2)))
        elif kind == "owners":
            right, column = right
            wide = left.shape[-2] // 2
            specs.append(
                pl.BlockSpec((None, tall, tokens), lambda k, place: (source(k, place), 0, 0))
            )
            specs.append(
                pl.BlockSpec(
                    (None, tokens, wide),
                    lambda k, place, column=column: (
                        source(k, place),
                        0,
                        2 * column + target(k, place) % 2,
                    ),
                )
            )
        else:
            wide = right.shape[1] // 8
            specs.append(pl.BlockSpec((tall, tokens), lambda k, place: (0, 0)))
            specs.append(pl.BlockSpec((tokens, wide), lambda k, place: (0, target(k, place))))
        arrays += [left, right]
        rows += tall
    return pl.pallas_call(
        half_kernel,
        out_shape=jax.ShapeDtypeStruct((4, rows, wide), BF),
        grid_spec=pltpu.PrefetchScalarGridSpec(
            num_scalar_prefetch=1,
            grid=(4,),
            in_specs=specs,
            out_specs=pl.BlockSpec((1, rows, wide), lambda k, place: (k, 0, 0)),
        ),
        compiler_params=pltpu.CompilerParams(vmem_limit_bytes=48 << 20),
        cost_estimate=cost(rows / 210),
    )(place, *arrays)


def turn_kernel(*refs):
    start = 0
    for block in refs[:-1]:
        rows = block.shape[0]
        refs[-1][:, pl.ds(start, rows)] = block[...].T
        start += rows


def turn(*blocks):
    width = blocks[0].shape[1]
    step = 512 if width % 512 == 0 else width
    rows = sum(block.shape[0] for block in blocks)
    return pl.pallas_call(
        turn_kernel,
        out_shape=jax.ShapeDtypeStruct((width, rows), BF),
        grid=(width // step,),
        in_specs=[pl.BlockSpec((block.shape[0], step), lambda i: (0, i)) for block in blocks],
        out_specs=pl.BlockSpec((step, rows), lambda i: (i, 0)),
        compiler_params=pltpu.CompilerParams(vmem_limit_bytes=32 << 20),
        cost_estimate=cost(3),
    )(*blocks)


def turn_own_kernel(place, *refs):
    blocks, out_ref = refs[:-1], refs[-1]
    rows = blocks[0].shape[0]
    for k, block in enumerate(blocks):
        turned = block[...].T
        for r in range(GROUP):
            out_ref[r, :, pl.ds((k ^ r) * rows, rows)] = turned


def turn_own(place, blocks, width):
    rows = blocks[0].shape[0]
    out = (GROUP, width, GROUP * rows)
    return pl.pallas_call(
        turn_own_kernel,
        out_shape=jax.ShapeDtypeStruct(out, BF),
        grid_spec=pltpu.PrefetchScalarGridSpec(
            num_scalar_prefetch=1,
            grid=(1,),
            in_specs=[pl.BlockSpec((rows, width), lambda i, place: (0, place[0]))] * GROUP,
            out_specs=pl.BlockSpec(out, lambda i, place: (0, 0, 0)),
        ),
        compiler_params=pltpu.CompilerParams(vmem_limit_bytes=32 << 20),
        cost_estimate=cost(3),
    )(place, *blocks)


def join_kernel(place, *refs):
    for r, block in enumerate(refs[:-1]):

        @pl.when(pl.program_id(0) == r)
        def _():
            refs[-1][...] = block[...]


def join(place, blocks):
    rows, width = blocks[0].shape
    return pl.pallas_call(
        join_kernel,
        out_shape=jax.ShapeDtypeStruct((GROUP * rows, width), BF),
        grid_spec=pltpu.PrefetchScalarGridSpec(
            num_scalar_prefetch=1,
            grid=(GROUP,),
            in_specs=[fixed(block) for block in blocks],
            out_specs=pl.BlockSpec((rows, width), lambda i, place: (place[0] ^ i, 0)),
        ),
        compiler_params=pltpu.CompilerParams(vmem_limit_bytes=40 << 20),
        cost_estimate=cost(5),
    )(place, *blocks)


def all_grads(parts, terms):
    rows = sum(left.shape[0] for left, right in terms)
    wide = terms[0][1].shape[1] // parts
    specs = []
    for left, right in terms:
        specs.append(pl.BlockSpec(left.shape, lambda p, place: (0, 0)))
        specs.append(pl.BlockSpec((right.shape[0], wide), lambda p, place: (0, p)))
    return pl.pallas_call(
        half_kernel,
        out_shape=jax.ShapeDtypeStruct((parts, rows, wide), BF),
        grid_spec=pltpu.PrefetchScalarGridSpec(
            num_scalar_prefetch=1,
            grid=(parts,),
            in_specs=specs,
            out_specs=pl.BlockSpec((1, rows, wide), lambda p, place: (p, 0, 0)),
        ),
        compiler_params=pltpu.CompilerParams(vmem_limit_bytes=48 << 20),
        cost_estimate=cost(18),
    )(jnp.zeros((2,), jnp.int32), *[array for term in terms for array in term])


def after(values, *earlier):
    return lax.optimization_barrier((values, *earlier))[0]


def wide_sum(*terms):
    total = terms[0].astype(F32)
    for term in terms[1:]:
        total = total + term.astype(F32)
    return total


def solution(mesh):
    dp, fsdp = mesh.shape["dp"], mesh.shape["fsdp"]
    assert fsdp == GROUP and dp % GROUP == 0
    inner = dp // GROUP

    def swap(values, r):
        return lax.ppermute(values, "fsdp", [(i, i ^ r) for i in range(fsdp)])

    def across(values):
        return lax.ppermute(values, "dp", [(i, i ^ 1) for i in range(dp)])

    def gather_blocks(values, chip=None):
        chip = swap(values, 2) if chip is None else chip
        return values, swap(values, 1), chip, swap(chip, 1)

    def gather_rows(values, chip=None):
        return jnp.concatenate(gather_blocks(values, chip), axis=0)

    def core_sum(terms):
        blocks = terms.reshape((GROUP, -1) + terms.shape[1:])
        got = swap(low(blocks[1::2]), 1)
        return wide_sum(blocks[0], got[0]), low(wide_sum(blocks[2], got[1]))

    def scatter_sum(terms):
        own, other = core_sum(terms)
        return own + swap(other, 2).astype(F32)

    def gather_plane(values, near=None):
        half = values.shape[0] // 2
        chip, side = near or (swap(values, 2), across(values))
        far = jnp.concatenate([across(chip[:half]), swap(side[half:], 2)], axis=0)
        blocks = [values, chip, side, far]
        mates = [swap(block, 1) for block in blocks]
        return jnp.concatenate([b for pair in zip(blocks, mates) for b in pair], axis=0)

    def plane_core(terms):
        blocks = terms.reshape((2 * GROUP, -1) + terms.shape[1:])
        got = swap(low(blocks[1::2]), 1)
        return [wide_sum(blocks[2 * i], got[i]) for i in range(GROUP)]

    def plane_far(sums):
        own, chip, side, far = sums
        half = far.shape[0] // 2
        top, bottom = across(low(far[:half])), swap(low(far[half:]), 2)
        chip = jnp.concatenate([wide_sum(chip[:half], top), chip[half:]], axis=0)
        side = jnp.concatenate([side[:half], wide_sum(side[half:], bottom)], axis=0)
        return own, low(chip), low(side)

    def plane_near(sums):
        own, chip, side = sums
        return own, swap(chip, 2), across(side)

    def pick(bit, low_part, high_part, axis):
        return jnp.where(
            bit == 0,
            jnp.concatenate([low_part, high_part], axis=axis),
            jnp.concatenate([high_part, low_part], axis=axis),
        )

    def sent_parts(weights, f, place, parts):
        rows, width = weights[0].shape[0], weights[0].shape[1] // GROUP
        size = rows // parts

        def part(weight, r):
            return lax.dynamic_slice(weight, (place * size, (f ^ r) * width), (size, width))

        return jnp.stack([jnp.stack([part(weight, 2), part(weight, 3)]) for weight in weights])

    def mate_parts(weights, f):
        rows, width = weights[0].shape[0], weights[0].shape[1] // GROUP
        sent = [lax.dynamic_slice(w, (0, (f ^ 1) * width), (rows, width)) for w in weights]
        return swap(jnp.stack(sent), 1)

    def head_pieces(weights, near, far, mate, mate_at=0):
        near_mate, far_mate = swap(near[:, 1], 1), swap(far[:, 1], 1)
        return [
            (
                weight,
                (mate, (i + mate_at,)),
                (near, (i, 0)),
                (far, (i, 0)),
                (near_mate, (i,)),
                (far_mate, (i,)),
            )
            for i, weight in enumerate(weights)
        ]

    def plain_sum(terms):
        parts = []
        for kind, left, right in terms:
            if kind == "owners":
                f = lax.axis_index("fsdp")
                size = left.shape[-2]
                right = right[0][:, :, right[1] * size : (right[1] + 1) * size]
                part = jnp.einsum("srt,stc->src", left, right, preferred_element_type=F32)
                part = jnp.take(part, f ^ jnp.arange(GROUP), axis=0)
                part = part.reshape(GROUP, size, inner, -1).transpose(0, 2, 1, 3)
                parts.append(low(part).reshape((dp, size, -1)))
            elif kind == "columns":
                tall = left.reshape(GROUP, -1, left.shape[1])
                wide = right.reshape(right.shape[0], inner, -1)
                part = jnp.einsum("zrt,txc->zxrc", tall, wide, preferred_element_type=F32)
                parts.append(low(part).reshape((dp,) + part.shape[2:]))
            else:
                wide = right.reshape(right.shape[0], dp, -1)
                parts.append(low(jnp.einsum("rt,tpc->prc", left, wide, preferred_element_type=F32)))
        grads = jnp.concatenate(parts, axis=1)
        return lax.psum_scatter(grads, "dp", scatter_dimension=0).astype(F32)

    def hop(values, bit):
        return lax.ppermute(values, "dp", [(i, i ^ (1 << bit)) for i in range(dp)])

    class Sum:
        def __init__(self, place, terms, order):
            self.place, self.terms, self.order = place, terms, order

        def send(self):
            if dp == 8:
                self.sent = half_grads(self.place, self.terms, self.order, 1)
            else:
                self.sent = self.total = plain_sum(self.terms)
            return self.sent

        def keep(self, *earlier):
            if dp == 8:
                first = after(self.terms[0][1], *earlier)
                terms = ((self.terms[0][0], first, self.terms[0][2]),) + self.terms[1:]
                self.kept = half_grads(self.place, terms, self.order, 0)
                return self.kept
            return self.sent

        def add(self, stage, *earlier):
            if dp != 8:
                return self.sent
            if stage == 1:
                self.one = after(hop(self.sent, self.order[0]), *earlier)
                self.sent = low(wide_sum(self.kept[2:], self.one[2:]))
                return self.sent
            if stage == 2:
                self.two = after(hop(self.sent, self.order[1]), *earlier)
                self.sent = low(wide_sum(self.kept[1], self.one[1], self.two[1]))
                return self.sent
            three = after(hop(self.sent, self.order[2]), *earlier)
            self.total = wide_sum(self.kept[0], self.one[0], self.two[0], three)
            return self.total

        def parts(self):
            out, at = [], 0
            for kind, left, right in self.terms:
                rows = left.shape[0] // GROUP if kind == "columns" else left.shape[-2]
                out.append(self.total[at : at + rows])
                at += rows
            return out

    def place_columns(values):
        pairs = []
        for z in range(GROUP):
            for x in range(inner):
                for f in range(GROUP):
                    pairs.append(((z * inner + x) * GROUP + f, (f * inner + x) * GROUP + z))
        return lax.ppermute(values, ("dp", "fsdp"), pairs)

    def on_device(
        tokens,
        patches,
        cotangent,
        lengths,
        episode_flags,
        norm_gains,
        w_query,
        w_key,
        w_value,
        w_out,
        c_query,
        c_key,
        c_value,
        c_out,
        patch_proj,
        w_gate,
        w_up,
        w_down,
    ):
        f = lax.axis_index("fsdp")
        x = lax.axis_index("dp") % 2
        z = (lax.axis_index("dp") // 2) % 2
        place = jnp.stack([f, lax.axis_index("dp")]).astype(jnp.int32)
        slot = tokens.shape[1]
        keys = patches.shape[1]
        width = tokens.shape[2] // GROUP
        inputs = tokens[0].astype(F32)
        bucket = jnp.where(
            lengths[0] <= slot // 4,
            slot // 4,
            jnp.where(lengths[0] <= slot // 2, slot // 2, slot),
        )
        live = (jnp.arange(slot, dtype=jnp.int32) < bucket).astype(F32)[:, None]
        grad_out = low(cotangent[0].astype(F32) * live)
        info = jnp.stack([lengths, episode_flags], axis=1)
        chip_info = swap(info, 2)
        w_query, w_key, w_value, inputs, chip_info = lax.optimization_barrier(
            (w_query, w_key, w_value, inputs, chip_info)
        )
        pair_near = swap(sent_parts((w_query, w_key), f, x, 2), 2)
        value_near = swap(sent_parts((w_value,), f, x, 2), 2)
        first = normed(inputs, norm_gains[0])
        first_chip = swap(first, 2)
        pair_far = across(pair_near)
        value_far = across(after(value_near, pair_far))

        rows = patch_proj.shape[0] // 4
        patch_in = after(patch_proj, pair_near)
        patch_mate = swap(patch_in, 1)
        patch_part = swap(lax.dynamic_slice_in_dim(patch_in, (2 * x + z) * rows, rows, 0), 2)
        patch_half = pick(z, patch_part, hop(patch_part, 1), 0)
        patch_chip = pick(x, patch_half, across(patch_half), 0)
        patch_far = swap(patch_chip, 1)
        cross_own = (c_key, c_value, c_query)
        cross_ready = after(cross_own, patch_part, value_near)
        cross_part = swap(sent_parts(cross_ready, f, 2 * x + z, 4), 2)
        self_mate = mate_parts((w_query, w_key, w_value), f)
        first_blocks = gather_blocks(first, after(first_chip, pair_far))
        info = jnp.concatenate([info, swap(info, 1), chip_info, swap(chip_info, 1)], axis=0)
        query_w, key_w = head_pieces((w_query, w_key), pair_near, pair_far, self_mate)
        (value_w,) = head_pieces((w_value,), value_near, value_far, self_mate, 2)
        queries = to_heads(place, first_blocks, query_w)
        keys_all = to_heads(place, first_blocks, key_w)
        values_all = to_heads(place, first_blocks, value_w)
        cross_part = after(cross_part, values_all)
        cross_near = pick(z, cross_part, hop(cross_part, 1), 2)
        cross_far = across(cross_near)
        mixed = attend(info, queries, keys_all, values_all, slot, slot, width, True)
        own, other = core_sum(low(nn(mixed, w_out)))
        cross_mate = mate_parts(after(cross_own, other), f)
        sent_out = other
        other = swap(other, 2)
        after_self = inputs + own + other.astype(F32)
        second = normed(after_self, norm_gains[1])
        second_chip = swap(second, 2)
        patch_blocks = (patch_proj, patch_mate, patch_chip, patch_far)
        patch_mat = join(place, after(patch_blocks, sent_out))
        context = low(nn(after(patches[0], second), patch_mat))
        context_chip = swap(context, 2)
        second_chip, cross_far = lax.optimization_barrier((second_chip, cross_far))
        second_blocks = gather_blocks(second, second_chip)
        cross_key_w, cross_value_w, cross_query_w = head_pieces(
            cross_own, cross_near, cross_far, cross_mate
        )
        cross_q = to_heads(place, second_blocks, cross_query_w)
        context_blocks = gather_blocks(context, after(context_chip, cross_q))
        cross_k = to_heads(place, context_blocks, cross_key_w)
        cross_v = to_heads(place, context_blocks, cross_value_w)
        cross_mixed = attend(info, cross_q, cross_k, cross_v, slot, keys, width, False)
        grad_early = after(grad_out, context)
        cross_mixed, *grad_near = lax.optimization_barrier(
            (cross_mixed, swap(grad_early, 2), across(grad_early))
        )
        own, other = core_sum(low(nn(cross_mixed, c_out)))
        grad_all = gather_plane(grad_out, tuple(grad_near))
        other = after(swap(other, 2), grad_all)
        after_cross = after_self + own + other.astype(F32)
        third = normed(after_cross, norm_gains[2])
        third_all = gather_plane(third)
        patch_width = patch_proj.shape[0]
        patch_rows = after(patches[0], third_all)

        def patch_piece(r):
            return lax.dynamic_slice(patch_rows, (0, (f ^ r) * patch_width), (keys, patch_width))

        patch_pieces = [patch_piece(0)] + [swap(patch_piece(r), r) for r in range(1, GROUP)]

        units = w_gate.shape[0] // 2
        gate_half, up_half, down_half = (
            lax.dynamic_slice_in_dim(w, x * units, units, 0) for w in (w_gate, w_up, w_down)
        )
        gate = nt(third_all, gate_half)
        up = nt(third_all, up_half)
        value, slope = gelu_parts(gate)
        hidden = low(value * up)
        grad_hidden = nt(grad_all, down_half)
        grad_gate = low(grad_hidden * up * slope)
        grad_up = low(grad_hidden * value)
        grad_gate, *patch_pieces = lax.optimization_barrier((grad_gate, *patch_pieces))
        third_part = low(nn(grad_gate, gate_half) + nn(grad_up, up_half))
        sums = plane_far(plane_core(third_part))
        hidden_terms = tuple(
            (turn(after(left, third_part)), right)
            for left, right in ((grad_gate, third_all), (grad_up, third_all), (hidden, grad_all))
        )
        first_left = after(hidden_terms[0][0], sums[1], sums[2])
        hidden_terms = ((first_left, third_all),) + hidden_terms[1:]
        hidden_bundle = all_grads(dp // 2, hidden_terms)
        hidden_grads = lax.psum_scatter(
            hidden_bundle,
            "dp",
            scatter_dimension=0,
            axis_index_groups=[list(range(i, dp, 2)) for i in range(2)],
        )
        own, chip, side = plane_near(sums)
        grad_third = wide_sum(own, after(chip, hidden_bundle), side)

        grad_norm, gain_third = norm_back(after_cross, norm_gains[2], grad_third)
        grad_after_cross = grad_out.astype(F32) + grad_norm
        grad_cross_out = low(grad_after_cross)
        cross_turned = turn(after(cross_mixed, grad_third))
        second_turned = turn(*after(second_blocks, grad_third))
        grad_cross_all = gather_rows(
            grad_cross_out, after(swap(grad_cross_out, 2), cross_turned, second_turned)
        )
        grad_cross_mixed = low(nt(grad_cross_all, c_out))
        grad_cq, grad_ck, grad_cv = attend_back(
            info, cross_q, cross_k, cross_v, grad_cross_mixed, slot, keys, width, False
        )
        own, other = core_sum(from_heads(place, (grad_cq,), (cross_query_w,)))
        context_turned = turn(*after(context_blocks, grad_cq))
        sum_cross = Sum(
            place,
            (("rows", cross_turned, grad_cross_all), ("columns", second_turned, grad_cq)),
            (0, 1, 2),
        )
        grad_second = own + after(swap(other, 2), sum_cross.send(), context_turned).astype(F32)

        grad_norm, gain_second = norm_back(after_self, norm_gains[1], grad_second)
        grad_after_self = grad_after_cross + grad_norm
        grad_self_out = low(grad_after_self)
        self_chip = swap(grad_self_out, 2)
        mixed_turned = turn(after(mixed, grad_self_out))
        first_turned = turn_own(place, after(first_blocks, grad_self_out), width)
        grad_self_all = gather_rows(
            grad_self_out,
            after(self_chip, mixed_turned, first_turned, sum_cross.keep(grad_self_out)),
        )
        grad_mixed = low(nt(grad_self_all, w_out))
        grad_q, grad_k, grad_v = attend_back(
            info, queries, keys_all, values_all, grad_mixed, slot, slot, width, True
        )
        heads = jnp.concatenate([grad_q, grad_k, grad_v], axis=1)
        heads_chip = swap(heads, 2)
        self_part = from_heads(place, (grad_q, grad_k, grad_v), (query_w, key_w, value_w))
        own, other = core_sum(self_part)
        other = swap(other, 2)
        context_part = from_heads(
            place, (after(grad_ck, self_part), grad_cv), (cross_key_w, cross_value_w)
        )
        context_own, context_other = core_sum(context_part)
        context_other = swap(context_other, 2)
        cross_one = sum_cross.add(1, context_part)
        sum_context = Sum(
            place,
            (
                ("columns", context_turned, grad_ck),
                ("columns", context_turned, grad_cv),
                ("rows", after(mixed_turned, heads_chip), grad_self_all),
            ),
            (0, 1, 2),
        )
        grad_first = own + after(
            other, sum_context.send(), cross_one, hidden_grads
        ).astype(F32)
        grad_norm, gain_first = norm_back(inputs, norm_gains[0], grad_first)
        tokens_grad = (grad_after_self + grad_norm)[None]
        gains = jnp.stack([gain_first, gain_second, gain_third])
        heads_all = jnp.stack([heads, swap(heads, 1), heads_chip, swap(heads_chip, 1)])
        sum_self = Sum(
            place,
            (("owners", first_turned, (heads_all, 0)), ("owners", first_turned, (heads_all, 1))),
            (0, 1, 2),
        )
        sum_value = Sum(place, (("owners", first_turned, (heads_all, 2)),), (1, 0, 2))
        kept = sum_context.keep(sum_self.send(), sum_value.send())
        step = sum_cross.add(2, kept)
        patch_turned = turn(*after(tuple(patch_pieces), kept))
        grad_context = low(context_own + after(context_other, kept, patch_turned).astype(F32))
        context_chip = swap(grad_context, 2)
        for bit in reversed(range(2, dp.bit_length() - 1)):
            gains = gains + after(hop(gains, bit), patch_turned)
        gains = gains + after(hop(gains, 1), grad_context)
        kept = sum_self.keep(grad_context, gains), sum_value.keep(grad_context)
        value_one = sum_value.add(1, *kept)
        cross_all = sum_cross.add(3, value_one)
        context_one = sum_context.add(1, cross_all)
        context_chip = after(context_chip, context_one)
        grad_context_all = gather_rows(grad_context, context_chip)
        sum_patch = Sum(place, (("rows", patch_turned, grad_context_all),), (1, 0, 2))
        sum_patch.send()
        kept = sum_patch.keep(sum_patch.sent)
        out_part = low(nn(after(hidden, kept), down_half))
        sums = plane_core(out_part)
        patches_grad = nt(after(grad_context, kept), patch_mat)[None]
        step = sum_context.add(2, kept, out_part, patches_grad)
        step = sum_self.add(1, step)
        own, chip, side = plane_far(after(tuple(sums), step))
        step = sum_patch.add(1, step)
        step = sum_value.add(2, step)
        gains = gains + after(hop(after(gains, step), 0), chip, side)
        gains = gains + after(swap(gains, 2), chip)
        gains_grad = gains + after(swap(gains, 1), chip)
        step = sum_patch.add(2, step, chip, side, gains_grad)
        step = sum_self.add(2, step)
        columns = tokens.shape[2] // dp
        hidden_grads = after(hidden_grads, step)
        hidden_other = across(
            lax.dynamic_slice_in_dim(hidden_grads, (1 - x) * columns, columns, 1)
        )
        own, chip, side = plane_near((own, chip, side))
        step = sum_context.add(3, step)
        c_out_grad, c_query_grad = sum_cross.parts()
        c_key_grad, c_value_grad, w_out_grad = sum_context.parts()
        moved = place_columns(low(jnp.stack([c_query_grad, c_key_grad, c_value_grad])))
        step = sum_value.add(3, step, hidden_other)
        step = sum_self.add(3, step)
        out_tokens = low((after_cross + wide_sum(own, after(chip, step), side)) * live)[None]
        hidden_mine = lax.dynamic_slice_in_dim(hidden_grads, x * columns, columns, 1)
        hidden_mine, hidden_other = after((hidden_mine, hidden_other), step)

        def both_halves(i):
            mine, other = (
                half[i * units : (i + 1) * units] for half in (hidden_mine, hidden_other)
            )
            return jnp.where(
                x == 0,
                jnp.concatenate([mine, other], axis=0),
                jnp.concatenate([other, mine], axis=0),
            ).astype(F32)

        gate_grad, up_grad, down_grad = (both_halves(i) for i in range(3))
        step = sum_patch.add(3, step, gate_grad)
        c_query_grad, c_key_grad, c_value_grad = after(moved, step).astype(F32)

        w_query_grad, w_key_grad = sum_self.parts()
        (w_value_grad,), (patch_proj_grad,) = sum_value.parts(), sum_patch.parts()

        return (
            out_tokens,
            tokens_grad,
            patches_grad,
            gains_grad,
            w_query_grad,
            w_key_grad,
            w_value_grad,
            w_out_grad,
            c_query_grad,
            c_key_grad,
            c_value_grad,
            c_out_grad,
            patch_proj_grad,
            gate_grad,
            up_grad,
            down_grad,
        )

    both, rows, block = ("dp", "fsdp"), P("fsdp", None), P("fsdp", "dp")
    whole = P(both, None, None)
    return jax.shard_map(
        on_device,
        mesh=mesh,
        in_specs=(whole, whole, whole, P(both), P(both), P()) + (rows,) * 12,
        out_specs=(whole, whole, whole, P()) + (block,) * 12,
        check_vma=False,
    )
```

```python
import functools

import jax
import jax.numpy as jnp
from jax import lax
from jax.experimental import pallas as pl
from jax.experimental.pallas import tpu as pltpu
from jax.sharding import PartitionSpec as P

HD = 128
SCALE = HD ** (-0.5)
EPS = 1e-06
BF = jnp.bfloat16
F32 = jnp.float32
GROUP = 4


def cost(us):
    return pl.CostEstimate(
        flops=int(us * 8e8), bytes_accessed=int(us * 2e6), transcendentals=0
    )


def low(v):
    return v.astype(BF)


def dot(left, right, left_dim, right_dim):
    return lax.dot_general(
        left, right, (((left_dim,), (right_dim,)), ((), ())), preferred_element_type=F32
    )


def nn(left, right):
    return dot(left, right, 1, 0)


def nt(left, right):
    return dot(left, right, 1, 1)


def tn(left, right):
    return dot(left, right, 0, 0)


def normed(values, gain):
    return low(values * lax.rsqrt(jnp.mean(values * values, axis=-1, keepdims=True) + EPS) * gain)


def norm_back(values, gain, grad):
    scale = lax.rsqrt(jnp.mean(values * values, axis=-1, keepdims=True) + EPS)
    unit = values * scale
    weighted = grad * gain
    grad_values = scale * (weighted - unit * jnp.mean(weighted * unit, axis=-1, keepdims=True))
    return grad_values, jnp.sum(grad * unit, axis=0)


def gelu_parts(v):
    c = 0.7978845608028654
    t = jnp.tanh(c * (v + 0.044715 * (v * v * v)))
    value = 0.5 * v * (1.0 + t)
    slope = 0.5 * (1.0 + t) + 0.5 * v * (1.0 - t * t) * (c * (1.0 + 3 * 0.044715 * v * v))
    return value, slope


def allowed_at(info, rows, columns):
    length = info[pl.program_id(0), 0]
    flag = info[pl.program_id(0), 1]
    prefix = jnp.where(flag == 0, length // 2, 0)
    query = lax.broadcasted_iota(jnp.int32, (rows, columns), 0)
    key = lax.broadcasted_iota(jnp.int32, (rows, columns), 1)
    return (key < length) & ((key <= query) | (key < prefix))


def probabilities(q, k, allowed):
    scores = nt(q, k) * SCALE
    if allowed is not None:
        scores = jnp.where(allowed, scores, -1e30)
    weights = jnp.exp(scores - jnp.max(scores, axis=-1, keepdims=True))
    return weights / jnp.sum(weights, axis=-1, keepdims=True)


def attend_kernel(masked, info, q_ref, k_ref, v_ref, out_ref):
    allowed = allowed_at(info, q_ref.shape[0], k_ref.shape[0]) if masked else None
    for head in range(q_ref.shape[1] // HD):
        at = pl.ds(head * HD, HD)
        probs = probabilities(q_ref[:, at], k_ref[:, at], allowed)
        out_ref[:, at] = low(nn(low(probs), v_ref[:, at]))


def attend_back_kernel(masked, info, q_ref, k_ref, v_ref, g_ref, gq_ref, gk_ref, gv_ref):
    allowed = allowed_at(info, q_ref.shape[0], k_ref.shape[0]) if masked else None
    for head in range(q_ref.shape[1] // HD):
        at = pl.ds(head * HD, HD)
        q, k, v, g = q_ref[:, at], k_ref[:, at], v_ref[:, at], g_ref[:, at]
        probs = probabilities(q, k, allowed)
        grad_probs = nt(g, v)
        gv_ref[:, at] = low(tn(low(probs), g))
        total = jnp.sum(probs * grad_probs, axis=-1, keepdims=True)
        grad_scores = low(probs * (grad_probs - total))
        gq_ref[:, at] = low(nn(grad_scores, k) * SCALE)
        gk_ref[:, at] = low(tn(grad_scores, q) * SCALE)


def head_block(rows, width):
    return pl.BlockSpec((rows, width), lambda s, info: (s, 0))


def attend(info, q, k, v, rows, keys, width, masked):
    return pl.pallas_call(
        functools.partial(attend_kernel, masked),
        out_shape=jax.ShapeDtypeStruct((GROUP * rows, width), BF),
        grid_spec=pltpu.PrefetchScalarGridSpec(
            num_scalar_prefetch=1,
            grid=(GROUP,),
            in_specs=[
                head_block(rows, width),
                head_block(keys, width),
                head_block(keys, width),
            ],
            out_specs=head_block(rows, width),
        ),
        compiler_params=pltpu.CompilerParams(vmem_limit_bytes=24 << 20),
        cost_estimate=cost(6 if masked else 4),
    )(info, q, k, v)


def attend_back(info, q, k, v, grad, rows, keys, width, masked):
    return pl.pallas_call(
        functools.partial(attend_back_kernel, masked),
        out_shape=(
            jax.ShapeDtypeStruct((GROUP * rows, width), BF),
            jax.ShapeDtypeStruct((GROUP * keys, width), BF),
            jax.ShapeDtypeStruct((GROUP * keys, width), BF),
        ),
        grid_spec=pltpu.PrefetchScalarGridSpec(
            num_scalar_prefetch=1,
            grid=(GROUP,),
            in_specs=[
                head_block(rows, width),
                head_block(keys, width),
                head_block(keys, width),
                head_block(rows, width),
            ],
            out_specs=(
                head_block(rows, width),
                head_block(keys, width),
                head_block(keys, width),
            ),
        ),
        compiler_params=pltpu.CompilerParams(vmem_limit_bytes=24 << 20),
        cost_estimate=cost(8),
    )(info, q, k, v, grad)


def placed(place, pieces):
    rows = pieces[0].shape[0]
    half = rows // 2
    f, x = place[0], place[1] % 2

    def at(block, part):
        return pl.multiple_of((f ^ block) * rows + part * half, half)

    spots = (
        pl.ds(at(0, 0), rows),
        pl.ds(at(1, 0), rows),
        pl.ds(at(2, x), half),
        pl.ds(at(2, 1 - x), half),
        pl.ds(at(3, x), half),
        pl.ds(at(3, 1 - x), half),
    )
    return tuple(zip(pieces, spots))


def row_tiles(rows, body):
    size = next((size for size in (512, 640) if rows % size == 0), rows)
    if size == rows:
        body(pl.ds(0, rows))
    else:
        pl.loop(0, rows // size)(lambda i: body(pl.ds(pl.multiple_of(i * size, size), size)))


def to_heads_kernel(count, place, *refs):
    pieces, out_ref = placed(place, refs[count : count + 6]), refs[count + 6]
    start = 0
    for rows_ref in refs[:count]:
        total = None
        for piece, features in pieces:
            term = nn(rows_ref[:, features], piece[...])
            total = term if total is None else total + term
        out_ref[pl.ds(start, rows_ref.shape[0]), :] = low(total)
        start += rows_ref.shape[0]


def from_heads_kernel(count, place, *refs):
    grads, pieces, out_ref = refs[:count], refs[count:-1], refs[-1]

    def tile(at):
        for part in range(6):
            total = None
            for i in range(count):
                piece, features = placed(place, pieces[6 * i : 6 * i + 6])[part]
                term = nt(grads[i][at, :], piece[...])
                total = term if total is None else total + term
            out_ref[at, features] = low(total)

    row_tiles(out_ref.shape[0], tile)


def piece_specs(pieces):
    rows, width = pieces[0].shape[0], pieces[1][0].shape[-1]
    specs = [pl.BlockSpec((rows, width), lambda i, place: (0, place[0]))]
    for array, at in pieces[1:]:
        block = (None,) * len(at) + array.shape[len(at) :]
        specs.append(pl.BlockSpec(block, lambda i, place, at=at: (*at, 0, 0)))
    return specs


def piece_arrays(pieces):
    return [pieces[0]] + [array for array, at in pieces[1:]]


def fixed(array):
    return pl.BlockSpec(array.shape, lambda i, place: (0, 0))


def to_heads(place, blocks, pieces):
    out = (sum(block.shape[0] for block in blocks), pieces[1][0].shape[-1])
    return pl.pallas_call(
        functools.partial(to_heads_kernel, len(blocks)),
        out_shape=jax.ShapeDtypeStruct(out, BF),
        grid_spec=pltpu.PrefetchScalarGridSpec(
            num_scalar_prefetch=1,
            grid=(1,),
            in_specs=[fixed(block) for block in blocks] + piece_specs(pieces),
            out_specs=pl.BlockSpec(out, lambda i, place: (0, 0)),
        ),
        compiler_params=pltpu.CompilerParams(vmem_limit_bytes=48 << 20),
        cost_estimate=cost(out[0] / 190),
    )(place, *blocks, *piece_arrays(pieces))


def from_heads(place, grads, weights):
    count = len(weights)
    out = (grads[0].shape[0], weights[0][0].shape[1])
    specs = [spec for pieces in weights for spec in piece_specs(pieces)]
    return pl.pallas_call(
        functools.partial(from_heads_kernel, count),
        out_shape=jax.ShapeDtypeStruct(out, BF),
        grid_spec=pltpu.PrefetchScalarGridSpec(
            num_scalar_prefetch=1,
            grid=(1,),
            in_specs=[fixed(g) for g in grads] + specs,
            out_specs=pl.BlockSpec(out, lambda i, place: (0, 0)),
        ),
        compiler_params=pltpu.CompilerParams(vmem_limit_bytes=56 << 20),
        cost_estimate=cost(3 + out[0] * count / 230),
    )(place, *grads, *[array for pieces in weights for array in piece_arrays(pieces)])


def half_kernel(place, *refs):
    lefts, rights, out_ref = refs[0:-1:2], refs[1:-1:2], refs[-1]
    start = 0
    for left, right in zip(lefts, rights):

        def product(at, start=start, left=left, right=right):
            out_ref[0, pl.ds(pl.multiple_of(start + at.start, 16), at.size), :] = low(
                nn(left[at, :], right[...])
            )

        row_tiles(left.shape[0], product)
        start += left.shape[0]


def half_grads(place, terms, order, side):
    def target(k, place):
        rel = (side << order[0]) + ((k // 2) << order[1]) + ((k % 2) << order[2])
        return place[1] ^ rel

    def source(k, place):
        return (target(k, place) // 2) ^ place[0]

    specs, arrays = [], []
    rows = 0
    for kind, left, right in terms:
        tall, tokens = left.shape[-2:]
        if kind == "columns":
            tall, wide = tall // GROUP, right.shape[1] // 2
            specs.append(pl.BlockSpec((tall, tokens), lambda k, place: (target(k, place) // 2, 0)))
            specs.append(pl.BlockSpec((tokens, wide), lambda k, place: (0, target(k, place) % 2)))
        elif kind == "owners":
            right, column = right
            wide = left.shape[-2] // 2
            specs.append(
                pl.BlockSpec((None, tall, tokens), lambda k, place: (source(k, place), 0, 0))
            )
            specs.append(
                pl.BlockSpec(
                    (None, tokens, wide),
                    lambda k, place, column=column: (
                        source(k, place),
                        0,
                        2 * column + target(k, place) % 2,
                    ),
                )
            )
        else:
            wide = right.shape[1] // 8
            specs.append(pl.BlockSpec((tall, tokens), lambda k, place: (0, 0)))
            specs.append(pl.BlockSpec((tokens, wide), lambda k, place: (0, target(k, place))))
        arrays += [left, right]
        rows += tall
    return pl.pallas_call(
        half_kernel,
        out_shape=jax.ShapeDtypeStruct((4, rows, wide), BF),
        grid_spec=pltpu.PrefetchScalarGridSpec(
            num_scalar_prefetch=1,
            grid=(4,),
            in_specs=specs,
            out_specs=pl.BlockSpec((1, rows, wide), lambda k, place: (k, 0, 0)),
        ),
        compiler_params=pltpu.CompilerParams(vmem_limit_bytes=48 << 20),
        cost_estimate=cost(rows / 210),
    )(place, *arrays)


def turn_kernel(*refs):
    start = 0
    for block in refs[:-1]:
        rows = block.shape[0]
        refs[-1][:, pl.ds(start, rows)] = block[...].T
        start += rows


def turn(*blocks):
    width = blocks[0].shape[1]
    step = 512 if width % 512 == 0 else width
    rows = sum(block.shape[0] for block in blocks)
    return pl.pallas_call(
        turn_kernel,
        out_shape=jax.ShapeDtypeStruct((width, rows), BF),
        grid=(width // step,),
        in_specs=[pl.BlockSpec((block.shape[0], step), lambda i: (0, i)) for block in blocks],
        out_specs=pl.BlockSpec((step, rows), lambda i: (i, 0)),
        compiler_params=pltpu.CompilerParams(vmem_limit_bytes=32 << 20),
        cost_estimate=cost(3),
    )(*blocks)


def turn_own_kernel(place, *refs):
    blocks, out_ref = refs[:-1], refs[-1]
    rows = blocks[0].shape[0]
    for k, block in enumerate(blocks):
        turned = block[...].T
        for r in range(GROUP):
            out_ref[r, :, pl.ds((k ^ r) * rows, rows)] = turned


def turn_own(place, blocks, width):
    rows = blocks[0].shape[0]
    out = (GROUP, width, GROUP * rows)
    return pl.pallas_call(
        turn_own_kernel,
        out_shape=jax.ShapeDtypeStruct(out, BF),
        grid_spec=pltpu.PrefetchScalarGridSpec(
            num_scalar_prefetch=1,
            grid=(1,),
            in_specs=[pl.BlockSpec((rows, width), lambda i, place: (0, place[0]))] * GROUP,
            out_specs=pl.BlockSpec(out, lambda i, place: (0, 0, 0)),
        ),
        compiler_params=pltpu.CompilerParams(vmem_limit_bytes=32 << 20),
        cost_estimate=cost(3),
    )(place, *blocks)


def join_kernel(place, *refs):
    for r, block in enumerate(refs[:-1]):

        @pl.when(pl.program_id(0) == r)
        def _():
            refs[-1][...] = block[...]


def join(place, blocks):
    rows, width = blocks[0].shape
    return pl.pallas_call(
        join_kernel,
        out_shape=jax.ShapeDtypeStruct((GROUP * rows, width), BF),
        grid_spec=pltpu.PrefetchScalarGridSpec(
            num_scalar_prefetch=1,
            grid=(GROUP,),
            in_specs=[fixed(block) for block in blocks],
            out_specs=pl.BlockSpec((rows, width), lambda i, place: (place[0] ^ i, 0)),
        ),
        compiler_params=pltpu.CompilerParams(vmem_limit_bytes=40 << 20),
        cost_estimate=cost(5),
    )(place, *blocks)


def all_grads(parts, terms):
    rows = sum(left.shape[0] for left, right in terms)
    wide = terms[0][1].shape[1] // parts
    specs = []
    for left, right in terms:
        specs.append(pl.BlockSpec(left.shape, lambda p, place: (0, 0)))
        specs.append(pl.BlockSpec((right.shape[0], wide), lambda p, place: (0, p)))
    return pl.pallas_call(
        half_kernel,
        out_shape=jax.ShapeDtypeStruct((parts, rows, wide), BF),
        grid_spec=pltpu.PrefetchScalarGridSpec(
            num_scalar_prefetch=1,
            grid=(parts,),
            in_specs=specs,
            out_specs=pl.BlockSpec((1, rows, wide), lambda p, place: (p, 0, 0)),
        ),
        compiler_params=pltpu.CompilerParams(vmem_limit_bytes=48 << 20),
        cost_estimate=cost(18),
    )(jnp.zeros((2,), jnp.int32), *[array for term in terms for array in term])


def after(values, *earlier):
    return lax.optimization_barrier((values, *earlier))[0]


def wide_sum(*terms):
    total = terms[0].astype(F32)
    for term in terms[1:]:
        total = total + term.astype(F32)
    return total


def solution(mesh):
    dp, fsdp = mesh.shape["dp"], mesh.shape["fsdp"]
    assert fsdp == GROUP and dp % GROUP == 0
    inner = dp // GROUP

    def swap(values, r):
        return lax.ppermute(values, "fsdp", [(i, i ^ r) for i in range(fsdp)])

    def across(values):
        return lax.ppermute(values, "dp", [(i, i ^ 1) for i in range(dp)])

    def gather_blocks(values, chip=None):
        chip = swap(values, 2) if chip is None else chip
        return values, swap(values, 1), chip, swap(chip, 1)

    def gather_rows(values, chip=None):
        return jnp.concatenate(gather_blocks(values, chip), axis=0)

    def core_sum(terms):
        blocks = terms.reshape((GROUP, -1) + terms.shape[1:])
        got = swap(low(blocks[1::2]), 1)
        return wide_sum(blocks[0], got[0]), low(wide_sum(blocks[2], got[1]))

    def scatter_sum(terms):
        own, other = core_sum(terms)
        return own + swap(other, 2).astype(F32)

    def gather_plane(values, near=None):
        half = values.shape[0] // 2
        chip, side = near or (swap(values, 2), across(values))
        far = jnp.concatenate([across(chip[:half]), swap(side[half:], 2)], axis=0)
        blocks = [values, chip, side, far]
        mates = [swap(block, 1) for block in blocks]
        return jnp.concatenate([b for pair in zip(blocks, mates) for b in pair], axis=0)

    def plane_core(terms):
        blocks = terms.reshape((2 * GROUP, -1) + terms.shape[1:])
        got = swap(low(blocks[1::2]), 1)
        return [wide_sum(blocks[2 * i], got[i]) for i in range(GROUP)]

    def plane_far(sums):
        own, chip, side, far = sums
        half = far.shape[0] // 2
        top, bottom = across(low(far[:half])), swap(low(far[half:]), 2)
        chip = jnp.concatenate([wide_sum(chip[:half], top), chip[half:]], axis=0)
        side = jnp.concatenate([side[:half], wide_sum(side[half:], bottom)], axis=0)
        return own, low(chip), low(side)

    def plane_near(sums):
        own, chip, side = sums
        return own, swap(chip, 2), across(side)

    def pick(bit, low_part, high_part, axis):
        return jnp.where(
            bit == 0,
            jnp.concatenate([low_part, high_part], axis=axis),
            jnp.concatenate([high_part, low_part], axis=axis),
        )

    def sent_parts(weights, f, place, parts):
        rows, width = weights[0].shape[0], weights[0].shape[1] // GROUP
        size = rows // parts

        def part(weight, r):
            return lax.dynamic_slice(weight, (place * size, (f ^ r) * width), (size, width))

        return jnp.stack([jnp.stack([part(weight, 2), part(weight, 3)]) for weight in weights])

    def mate_parts(weights, f):
        rows, width = weights[0].shape[0], weights[0].shape[1] // GROUP
        sent = [lax.dynamic_slice(w, (0, (f ^ 1) * width), (rows, width)) for w in weights]
        return swap(jnp.stack(sent), 1)

    def head_pieces(weights, near, far, mate, mate_at=0):
        near_mate, far_mate = swap(near[:, 1], 1), swap(far[:, 1], 1)
        return [
            (
                weight,
                (mate, (i + mate_at,)),
                (near, (i, 0)),
                (far, (i, 0)),
                (near_mate, (i,)),
                (far_mate, (i,)),
            )
            for i, weight in enumerate(weights)
        ]

    def plain_sum(terms):
        parts = []
        for kind, left, right in terms:
            if kind == "owners":
                f = lax.axis_index("fsdp")
                size = left.shape[-2]
                right = right[0][:, :, right[1] * size : (right[1] + 1) * size]
                part = jnp.einsum("srt,stc->src", left, right, preferred_element_type=F32)
                part = jnp.take(part, f ^ jnp.arange(GROUP), axis=0)
                part = part.reshape(GROUP, size, inner, -1).transpose(0, 2, 1, 3)
                parts.append(low(part).reshape((dp, size, -1)))
            elif kind == "columns":
                tall = left.reshape(GROUP, -1, left.shape[1])
                wide = right.reshape(right.shape[0], inner, -1)
                part = jnp.einsum("zrt,txc->zxrc", tall, wide, preferred_element_type=F32)
                parts.append(low(part).reshape((dp,) + part.shape[2:]))
            else:
                wide = right.reshape(right.shape[0], dp, -1)
                parts.append(low(jnp.einsum("rt,tpc->prc", left, wide, preferred_element_type=F32)))
        grads = jnp.concatenate(parts, axis=1)
        return lax.psum_scatter(grads, "dp", scatter_dimension=0).astype(F32)

    def hop(values, bit):
        return lax.ppermute(values, "dp", [(i, i ^ (1 << bit)) for i in range(dp)])

    class Sum:
        def __init__(self, place, terms, order):
            self.place, self.terms, self.order = place, terms, order

        def send(self):
            if dp == 8:
                self.sent = half_grads(self.place, self.terms, self.order, 1)
            else:
                self.sent = self.total = plain_sum(self.terms)
            return self.sent

        def keep(self, *earlier):
            if dp == 8:
                first = after(self.terms[0][1], *earlier)
                terms = ((self.terms[0][0], first, self.terms[0][2]),) + self.terms[1:]
                self.kept = half_grads(self.place, terms, self.order, 0)
                return self.kept
            return self.sent

        def add(self, stage, *earlier):
            if dp != 8:
                return self.sent
            if stage == 1:
                self.one = after(hop(self.sent, self.order[0]), *earlier)
                self.sent = low(wide_sum(self.kept[2:], self.one[2:]))
                return self.sent
            if stage == 2:
                self.two = after(hop(self.sent, self.order[1]), *earlier)
                self.sent = low(wide_sum(self.kept[1], self.one[1], self.two[1]))
                return self.sent
            three = after(hop(self.sent, self.order[2]), *earlier)
            self.total = wide_sum(self.kept[0], self.one[0], self.two[0], three)
            return self.total

        def parts(self):
            out, at = [], 0
            for kind, left, right in self.terms:
                rows = left.shape[0] // GROUP if kind == "columns" else left.shape[-2]
                out.append(self.total[at : at + rows])
                at += rows
            return out

    def place_columns(values):
        pairs = []
        for z in range(GROUP):
            for x in range(inner):
                for f in range(GROUP):
                    pairs.append(((z * inner + x) * GROUP + f, (f * inner + x) * GROUP + z))
        return lax.ppermute(values, ("dp", "fsdp"), pairs)

    def on_device(
        tokens,
        patches,
        cotangent,
        lengths,
        episode_flags,
        norm_gains,
        w_query,
        w_key,
        w_value,
        w_out,
        c_query,
        c_key,
        c_value,
        c_out,
        patch_proj,
        w_gate,
        w_up,
        w_down,
    ):
        f = lax.axis_index("fsdp")
        x = lax.axis_index("dp") % 2
        z = (lax.axis_index("dp") // 2) % 2
        place = jnp.stack([f, lax.axis_index("dp")]).astype(jnp.int32)
        slot = tokens.shape[1]
        keys = patches.shape[1]
        width = tokens.shape[2] // GROUP
        inputs = tokens[0].astype(F32)
        bucket = jnp.where(
            lengths[0] <= slot // 4,
            slot // 4,
            jnp.where(lengths[0] <= slot // 2, slot // 2, slot),
        )
        live = (jnp.arange(slot, dtype=jnp.int32) < bucket).astype(F32)[:, None]
        grad_out = low(cotangent[0].astype(F32) * live)
        info = jnp.stack([lengths, episode_flags], axis=1)
        chip_info = swap(info, 2)
        w_query, w_key, w_value, inputs, chip_info = lax.optimization_barrier(
            (w_query, w_key, w_value, inputs, chip_info)
        )
        pair_near = swap(sent_parts((w_query, w_key), f, x, 2), 2)
        value_near = swap(sent_parts((w_value,), f, x, 2), 2)
        first = normed(inputs, norm_gains[0])
        first_chip = swap(first, 2)
        pair_far = across(pair_near)
        value_far = across(after(value_near, pair_far))

        rows = patch_proj.shape[0] // 4
        patch_in = after(patch_proj, pair_near)
        patch_mate = swap(patch_in, 1)
        patch_part = swap(lax.dynamic_slice_in_dim(patch_in, (2 * x + z) * rows, rows, 0), 2)
        patch_half = pick(z, patch_part, hop(patch_part, 1), 0)
        patch_chip = pick(x, patch_half, across(patch_half), 0)
        patch_far = swap(patch_chip, 1)
        cross_own = (c_key, c_value, c_query)
        cross_ready = after(cross_own, patch_part, value_near)
        cross_part = swap(sent_parts(cross_ready, f, 2 * x + z, 4), 2)
        cross_near = pick(z, cross_part, hop(cross_part, 1), 2)
        cross_far = across(cross_near)
        self_mate = mate_parts((w_query, w_key, w_value), f)
        first_blocks = gather_blocks(first, after(first_chip, pair_far))
        info = jnp.concatenate([info, swap(info, 1), chip_info, swap(chip_info, 1)], axis=0)
        query_w, key_w = head_pieces((w_query, w_key), pair_near, pair_far, self_mate)
        (value_w,) = head_pieces((w_value,), value_near, value_far, self_mate, 2)
        queries = to_heads(place, first_blocks, query_w)
        keys_all = to_heads(place, first_blocks, key_w)
        values_all = to_heads(place, first_blocks, value_w)
        mixed = attend(info, queries, keys_all, values_all, slot, slot, width, True)
        own, other = core_sum(low(nn(after(mixed, cross_near, patch_half), w_out)))
        cross_mate = mate_parts(after(cross_own, other), f)
        sent_out = other
        other = swap(other, 2)
        after_self = inputs + own + other.astype(F32)
        second = normed(after_self, norm_gains[1])
        second_chip = swap(second, 2)
        patch_blocks = (patch_proj, patch_mate, patch_chip, patch_far)
        patch_mat = join(place, after(patch_blocks, sent_out))
        context = low(nn(after(patches[0], second), patch_mat))
        context_chip = swap(context, 2)
        second_chip, cross_far = lax.optimization_barrier((second_chip, cross_far))
        second_blocks = gather_blocks(second, second_chip)
        cross_key_w, cross_value_w, cross_query_w = head_pieces(
            cross_own, cross_near, cross_far, cross_mate
        )
        cross_q = to_heads(place, second_blocks, cross_query_w)
        context_blocks = gather_blocks(context, after(context_chip, cross_q))
        cross_k = to_heads(place, context_blocks, cross_key_w)
        cross_v = to_heads(place, context_blocks, cross_value_w)
        cross_mixed = attend(info, cross_q, cross_k, cross_v, slot, keys, width, False)
        grad_early = after(grad_out, context)
        cross_mixed, *grad_near = lax.optimization_barrier(
            (cross_mixed, swap(grad_early, 2), across(grad_early))
        )
        own, other = core_sum(low(nn(cross_mixed, c_out)))
        grad_all = gather_plane(grad_out, tuple(grad_near))
        other = after(swap(other, 2), grad_all)
        after_cross = after_self + own + other.astype(F32)
        third = normed(after_cross, norm_gains[2])
        third_all = gather_plane(third)
        patch_width = patch_proj.shape[0]
        patch_rows = after(patches[0], third_all)

        def patch_piece(r):
            return lax.dynamic_slice(patch_rows, (0, (f ^ r) * patch_width), (keys, patch_width))

        patch_pieces = [patch_piece(0)] + [swap(patch_piece(r), r) for r in range(1, GROUP)]

        units = w_gate.shape[0] // 2
        gate_half, up_half, down_half = (
            lax.dynamic_slice_in_dim(w, x * units, units, 0) for w in (w_gate, w_up, w_down)
        )
        gate = nt(third_all, gate_half)
        up = nt(third_all, up_half)
        value, slope = gelu_parts(gate)
        hidden = low(value * up)
        grad_hidden = nt(grad_all, down_half)
        grad_gate = low(grad_hidden * up * slope)
        grad_up = low(grad_hidden * value)
        grad_gate, *patch_pieces = lax.optimization_barrier((grad_gate, *patch_pieces))
        third_part = low(nn(grad_gate, gate_half) + nn(grad_up, up_half))
        sums = plane_far(plane_core(third_part))
        hidden_terms = tuple(
            (turn(after(left, third_part)), right)
            for left, right in ((grad_gate, third_all), (grad_up, third_all), (hidden, grad_all))
        )
        first_left = after(hidden_terms[0][0], sums[1], sums[2])
        hidden_terms = ((first_left, third_all),) + hidden_terms[1:]
        hidden_bundle = all_grads(dp // 2, hidden_terms)
        hidden_grads = lax.psum_scatter(
            hidden_bundle,
            "dp",
            scatter_dimension=0,
            axis_index_groups=[list(range(i, dp, 2)) for i in range(2)],
        )
        own, chip, side = plane_near(sums)
        grad_third = wide_sum(own, after(chip, hidden_bundle), side)

        grad_norm, gain_third = norm_back(after_cross, norm_gains[2], grad_third)
        grad_after_cross = grad_out.astype(F32) + grad_norm
        grad_cross_out = low(grad_after_cross)
        cross_turned = turn(after(cross_mixed, grad_third))
        second_turned = turn(*after(second_blocks, grad_third))
        grad_cross_all = gather_rows(
            grad_cross_out, after(swap(grad_cross_out, 2), cross_turned, second_turned)
        )
        grad_cross_mixed = low(nt(grad_cross_all, c_out))
        grad_cq, grad_ck, grad_cv = attend_back(
            info, cross_q, cross_k, cross_v, grad_cross_mixed, slot, keys, width, False
        )
        own, other = core_sum(from_heads(place, (grad_cq,), (cross_query_w,)))
        context_turned = turn(*after(context_blocks, grad_cq))
        sum_cross = Sum(
            place,
            (("rows", cross_turned, grad_cross_all), ("columns", second_turned, grad_cq)),
            (0, 1, 2),
        )
        grad_second = own + after(swap(other, 2), sum_cross.send(), context_turned).astype(F32)

        grad_norm, gain_second = norm_back(after_self, norm_gains[1], grad_second)
        grad_after_self = grad_after_cross + grad_norm
        grad_self_out = low(grad_after_self)
        self_chip = swap(grad_self_out, 2)
        mixed_turned = turn(after(mixed, grad_self_out))
        first_turned = turn_own(place, after(first_blocks, grad_self_out), width)
        grad_self_all = gather_rows(
            grad_self_out,
            after(self_chip, mixed_turned, first_turned, sum_cross.keep(grad_self_out)),
        )
        grad_mixed = low(nt(grad_self_all, w_out))
        grad_q, grad_k, grad_v = attend_back(
            info, queries, keys_all, values_all, grad_mixed, slot, slot, width, True
        )
        heads = jnp.concatenate([grad_q, grad_k, grad_v], axis=1)
        heads_chip = swap(heads, 2)
        self_part = from_heads(place, (grad_q, grad_k, grad_v), (query_w, key_w, value_w))
        own, other = core_sum(self_part)
        other = swap(other, 2)
        context_part = from_heads(
            place, (after(grad_ck, self_part), grad_cv), (cross_key_w, cross_value_w)
        )
        context_own, context_other = core_sum(context_part)
        context_other = swap(context_other, 2)
        cross_one = sum_cross.add(1, context_part)
        sum_context = Sum(
            place,
            (
                ("columns", context_turned, grad_ck),
                ("columns", context_turned, grad_cv),
                ("rows", after(mixed_turned, heads_chip), grad_self_all),
            ),
            (0, 1, 2),
        )
        grad_first = own + after(
            other, sum_context.send(), cross_one, hidden_grads
        ).astype(F32)
        grad_norm, gain_first = norm_back(inputs, norm_gains[0], grad_first)
        tokens_grad = (grad_after_self + grad_norm)[None]
        gains = jnp.stack([gain_first, gain_second, gain_third])
        heads_all = jnp.stack([heads, swap(heads, 1), heads_chip, swap(heads_chip, 1)])
        sum_self = Sum(
            place,
            (("owners", first_turned, (heads_all, 0)), ("owners", first_turned, (heads_all, 1))),
            (0, 1, 2),
        )
        sum_value = Sum(place, (("owners", first_turned, (heads_all, 2)),), (1, 0, 2))
        kept = sum_context.keep(sum_self.send(), sum_value.send())
        step = sum_cross.add(2, kept)
        patch_turned = turn(*after(tuple(patch_pieces), kept))
        grad_context = low(context_own + after(context_other, kept, patch_turned).astype(F32))
        context_chip = swap(grad_context, 2)
        for bit in reversed(range(2, dp.bit_length() - 1)):
            gains = gains + after(hop(gains, bit), patch_turned)
        gains = gains + after(hop(gains, 1), grad_context)
        kept = sum_self.keep(grad_context, gains), sum_value.keep(grad_context)
        value_one = sum_value.add(1, *kept)
        context_chip = after(context_chip, value_one, step)
        grad_context_all = gather_rows(grad_context, context_chip)
        sum_patch = Sum(place, (("rows", patch_turned, grad_context_all),), (1, 0, 2))
        sum_patch.send()
        kept = sum_patch.keep(sum_patch.sent)
        out_part = low(nn(after(hidden, kept), down_half))
        sums = plane_core(out_part)
        patches_grad = nt(after(grad_context, kept), patch_mat)[None]
        context_one = sum_context.add(1, kept, out_part, patches_grad)
        patch_one = sum_patch.add(1, context_one)
        step = sum_context.add(2, patch_one)
        step = sum_self.add(1, step)
        own, chip, side = plane_far(after(tuple(sums), step))
        step = sum_cross.add(3, step)
        step = sum_value.add(2, step)
        gains = gains + after(hop(after(gains, step), 0), chip, side)
        gains = gains + after(swap(gains, 2), chip)
        gains_grad = gains + after(swap(gains, 1), chip)
        step = sum_patch.add(2, step, chip, side, gains_grad)
        step = sum_self.add(2, step)
        columns = tokens.shape[2] // dp
        hidden_grads = after(hidden_grads, step)
        hidden_other = across(
            lax.dynamic_slice_in_dim(hidden_grads, (1 - x) * columns, columns, 1)
        )
        own, chip, side = plane_near((own, chip, side))
        step = sum_context.add(3, step)
        c_out_grad, c_query_grad = sum_cross.parts()
        c_key_grad, c_value_grad, w_out_grad = sum_context.parts()
        moved = place_columns(low(jnp.stack([c_query_grad, c_key_grad, c_value_grad])))
        step = sum_value.add(3, step, hidden_other)
        step = sum_self.add(3, step)
        out_tokens = low((after_cross + wide_sum(own, after(chip, step), side)) * live)[None]
        hidden_mine = lax.dynamic_slice_in_dim(hidden_grads, x * columns, columns, 1)
        hidden_mine, hidden_other = after((hidden_mine, hidden_other), step)

        def both_halves(i):
            mine, other = (
                half[i * units : (i + 1) * units] for half in (hidden_mine, hidden_other)
            )
            return jnp.where(
                x == 0,
                jnp.concatenate([mine, other], axis=0),
                jnp.concatenate([other, mine], axis=0),
            ).astype(F32)

        gate_grad, up_grad, down_grad = (both_halves(i) for i in range(3))
        step = sum_patch.add(3, step, gate_grad)
        c_query_grad, c_key_grad, c_value_grad = after(moved, step).astype(F32)

        w_query_grad, w_key_grad = sum_self.parts()
        (w_value_grad,), (patch_proj_grad,) = sum_value.parts(), sum_patch.parts()

        return (
            out_tokens,
            tokens_grad,
            patches_grad,
            gains_grad,
            w_query_grad,
            w_key_grad,
            w_value_grad,
            w_out_grad,
            c_query_grad,
            c_key_grad,
            c_value_grad,
            c_out_grad,
            patch_proj_grad,
            gate_grad,
            up_grad,
            down_grad,
        )

    both, rows, block = ("dp", "fsdp"), P("fsdp", None), P("fsdp", "dp")
    whole = P(both, None, None)
    return jax.shard_map(
        on_device,
        mesh=mesh,
        in_specs=(whole, whole, whole, P(both), P(both), P()) + (rows,) * 12,
        out_specs=(whole, whole, whole, P()) + (block,) * 12,
        check_vma=False,
    )
```

```python
import functools

import jax
import jax.numpy as jnp
from jax import lax
from jax.experimental import pallas as pl
from jax.experimental.pallas import tpu as pltpu
from jax.sharding import PartitionSpec as P

HD = 128
SCALE = HD ** (-0.5)
EPS = 1e-06
BF = jnp.bfloat16
F32 = jnp.float32
GROUP = 4


def cost(us):
    return pl.CostEstimate(
        flops=int(us * 8e8), bytes_accessed=int(us * 2e6), transcendentals=0
    )


def low(v):
    return v.astype(BF)


def dot(left, right, left_dim, right_dim):
    return lax.dot_general(
        left, right, (((left_dim,), (right_dim,)), ((), ())), preferred_element_type=F32
    )


def nn(left, right):
    return dot(left, right, 1, 0)


def nt(left, right):
    return dot(left, right, 1, 1)


def tn(left, right):
    return dot(left, right, 0, 0)


def normed(values, gain):
    return low(values * lax.rsqrt(jnp.mean(values * values, axis=-1, keepdims=True) + EPS) * gain)


def norm_back(values, gain, grad):
    scale = lax.rsqrt(jnp.mean(values * values, axis=-1, keepdims=True) + EPS)
    unit = values * scale
    weighted = grad * gain
    grad_values = scale * (weighted - unit * jnp.mean(weighted * unit, axis=-1, keepdims=True))
    return grad_values, jnp.sum(grad * unit, axis=0)


def gelu_parts(v):
    c = 0.7978845608028654
    t = jnp.tanh(c * (v + 0.044715 * (v * v * v)))
    value = 0.5 * v * (1.0 + t)
    slope = 0.5 * (1.0 + t) + 0.5 * v * (1.0 - t * t) * (c * (1.0 + 3 * 0.044715 * v * v))
    return value, slope


def allowed_at(info, rows, columns):
    length = info[pl.program_id(0), 0]
    flag = info[pl.program_id(0), 1]
    prefix = jnp.where(flag == 0, length // 2, 0)
    query = lax.broadcasted_iota(jnp.int32, (rows, columns), 0)
    key = lax.broadcasted_iota(jnp.int32, (rows, columns), 1)
    return (key < length) & ((key <= query) | (key < prefix))


def probabilities(q, k, allowed):
    scores = nt(q, k) * SCALE
    if allowed is not None:
        scores = jnp.where(allowed, scores, -1e30)
    weights = jnp.exp(scores - jnp.max(scores, axis=-1, keepdims=True))
    return weights / jnp.sum(weights, axis=-1, keepdims=True)


def attend_kernel(masked, info, q_ref, k_ref, v_ref, out_ref):
    allowed = allowed_at(info, q_ref.shape[0], k_ref.shape[0]) if masked else None
    for head in range(q_ref.shape[1] // HD):
        at = pl.ds(head * HD, HD)
        probs = probabilities(q_ref[:, at], k_ref[:, at], allowed)
        out_ref[:, at] = low(nn(low(probs), v_ref[:, at]))


def attend_back_kernel(masked, info, q_ref, k_ref, v_ref, g_ref, gq_ref, gk_ref, gv_ref):
    allowed = allowed_at(info, q_ref.shape[0], k_ref.shape[0]) if masked else None
    for head in range(q_ref.shape[1] // HD):
        at = pl.ds(head * HD, HD)
        q, k, v, g = q_ref[:, at], k_ref[:, at], v_ref[:, at], g_ref[:, at]
        probs = probabilities(q, k, allowed)
        grad_probs = nt(g, v)
        gv_ref[:, at] = low(tn(low(probs), g))
        total = jnp.sum(probs * grad_probs, axis=-1, keepdims=True)
        grad_scores = low(probs * (grad_probs - total))
        gq_ref[:, at] = low(nn(grad_scores, k) * SCALE)
        gk_ref[:, at] = low(tn(grad_scores, q) * SCALE)


def head_block(rows, width):
    return pl.BlockSpec((rows, width), lambda s, info: (s, 0))


def attend(info, q, k, v, rows, keys, width, masked):
    return pl.pallas_call(
        functools.partial(attend_kernel, masked),
        out_shape=jax.ShapeDtypeStruct((GROUP * rows, width), BF),
        grid_spec=pltpu.PrefetchScalarGridSpec(
            num_scalar_prefetch=1,
            grid=(GROUP,),
            in_specs=[
                head_block(rows, width),
                head_block(keys, width),
                head_block(keys, width),
            ],
            out_specs=head_block(rows, width),
        ),
        compiler_params=pltpu.CompilerParams(vmem_limit_bytes=24 << 20),
        cost_estimate=cost(6 if masked else 4),
    )(info, q, k, v)


def attend_back(info, q, k, v, grad, rows, keys, width, masked):
    return pl.pallas_call(
        functools.partial(attend_back_kernel, masked),
        out_shape=(
            jax.ShapeDtypeStruct((GROUP * rows, width), BF),
            jax.ShapeDtypeStruct((GROUP * keys, width), BF),
            jax.ShapeDtypeStruct((GROUP * keys, width), BF),
        ),
        grid_spec=pltpu.PrefetchScalarGridSpec(
            num_scalar_prefetch=1,
            grid=(GROUP,),
            in_specs=[
                head_block(rows, width),
                head_block(keys, width),
                head_block(keys, width),
                head_block(rows, width),
            ],
            out_specs=(
                head_block(rows, width),
                head_block(keys, width),
                head_block(keys, width),
            ),
        ),
        compiler_params=pltpu.CompilerParams(vmem_limit_bytes=24 << 20),
        cost_estimate=cost(8),
    )(info, q, k, v, grad)


def placed(place, pieces):
    rows = pieces[0].shape[0]
    half = rows // 2
    f, x = place[0], place[1] % 2

    def at(block, part):
        return pl.multiple_of((f ^ block) * rows + part * half, half)

    spots = (
        pl.ds(at(0, 0), rows),
        pl.ds(at(1, 0), rows),
        pl.ds(at(2, x), half),
        pl.ds(at(2, 1 - x), half),
        pl.ds(at(3, x), half),
        pl.ds(at(3, 1 - x), half),
    )
    return tuple(zip(pieces, spots))


def row_tiles(rows, body):
    size = next((size for size in (512, 640) if rows % size == 0), rows)
    if size == rows:
        body(pl.ds(0, rows))
    else:
        pl.loop(0, rows // size)(lambda i: body(pl.ds(pl.multiple_of(i * size, size), size)))


def to_heads_kernel(count, place, *refs):
    pieces, out_ref = placed(place, refs[count : count + 6]), refs[count + 6]
    start = 0
    for rows_ref in refs[:count]:
        total = None
        for piece, features in pieces:
            term = nn(rows_ref[:, features], piece[...])
            total = term if total is None else total + term
        out_ref[pl.ds(start, rows_ref.shape[0]), :] = low(total)
        start += rows_ref.shape[0]


def from_heads_kernel(count, place, *refs):
    grads, pieces, out_ref = refs[:count], refs[count:-1], refs[-1]

    def tile(at):
        for part in range(6):
            total = None
            for i in range(count):
                piece, features = placed(place, pieces[6 * i : 6 * i + 6])[part]
                term = nt(grads[i][at, :], piece[...])
                total = term if total is None else total + term
            out_ref[at, features] = low(total)

    row_tiles(out_ref.shape[0], tile)


def piece_specs(pieces):
    rows, width = pieces[0].shape[0], pieces[1][0].shape[-1]
    specs = [pl.BlockSpec((rows, width), lambda i, place: (0, place[0]))]
    for array, at in pieces[1:]:
        block = (None,) * len(at) + array.shape[len(at) :]
        specs.append(pl.BlockSpec(block, lambda i, place, at=at: (*at, 0, 0)))
    return specs


def piece_arrays(pieces):
    return [pieces[0]] + [array for array, at in pieces[1:]]


def fixed(array):
    return pl.BlockSpec(array.shape, lambda i, place: (0, 0))


def to_heads(place, blocks, pieces):
    out = (sum(block.shape[0] for block in blocks), pieces[1][0].shape[-1])
    return pl.pallas_call(
        functools.partial(to_heads_kernel, len(blocks)),
        out_shape=jax.ShapeDtypeStruct(out, BF),
        grid_spec=pltpu.PrefetchScalarGridSpec(
            num_scalar_prefetch=1,
            grid=(1,),
            in_specs=[fixed(block) for block in blocks] + piece_specs(pieces),
            out_specs=pl.BlockSpec(out, lambda i, place: (0, 0)),
        ),
        compiler_params=pltpu.CompilerParams(vmem_limit_bytes=48 << 20),
        cost_estimate=cost(out[0] / 190),
    )(place, *blocks, *piece_arrays(pieces))


def from_heads(place, grads, weights):
    count = len(weights)
    out = (grads[0].shape[0], weights[0][0].shape[1])
    specs = [spec for pieces in weights for spec in piece_specs(pieces)]
    return pl.pallas_call(
        functools.partial(from_heads_kernel, count),
        out_shape=jax.ShapeDtypeStruct(out, BF),
        grid_spec=pltpu.PrefetchScalarGridSpec(
            num_scalar_prefetch=1,
            grid=(1,),
            in_specs=[fixed(g) for g in grads] + specs,
            out_specs=pl.BlockSpec(out, lambda i, place: (0, 0)),
        ),
        compiler_params=pltpu.CompilerParams(vmem_limit_bytes=56 << 20),
        cost_estimate=cost(3 + out[0] * count / 230),
    )(place, *grads, *[array for pieces in weights for array in piece_arrays(pieces)])


def half_kernel(place, *refs):
    lefts, rights, out_ref = refs[0:-1:2], refs[1:-1:2], refs[-1]
    start = 0
    for left, right in zip(lefts, rights):

        def product(at, start=start, left=left, right=right):
            out_ref[0, pl.ds(pl.multiple_of(start + at.start, 16), at.size), :] = low(
                nn(left[at, :], right[...])
            )

        row_tiles(left.shape[0], product)
        start += left.shape[0]


def half_grads(place, terms, order, side):
    def target(k, place):
        rel = (side << order[0]) + ((k // 2) << order[1]) + ((k % 2) << order[2])
        return place[1] ^ rel

    def source(k, place):
        return (target(k, place) // 2) ^ place[0]

    specs, arrays = [], []
    rows = 0
    for kind, left, right in terms:
        tall, tokens = left.shape[-2:]
        if kind == "columns":
            tall, wide = tall // GROUP, right.shape[1] // 2
            specs.append(pl.BlockSpec((tall, tokens), lambda k, place: (target(k, place) // 2, 0)))
            specs.append(pl.BlockSpec((tokens, wide), lambda k, place: (0, target(k, place) % 2)))
        elif kind == "owners":
            right, column = right
            wide = left.shape[-2] // 2
            specs.append(
                pl.BlockSpec((None, tall, tokens), lambda k, place: (source(k, place), 0, 0))
            )
            specs.append(
                pl.BlockSpec(
                    (None, tokens, wide),
                    lambda k, place, column=column: (
                        source(k, place),
                        0,
                        2 * column + target(k, place) % 2,
                    ),
                )
            )
        else:
            wide = right.shape[1] // 8
            specs.append(pl.BlockSpec((tall, tokens), lambda k, place: (0, 0)))
            specs.append(pl.BlockSpec((tokens, wide), lambda k, place: (0, target(k, place))))
        arrays += [left, right]
        rows += tall
    return pl.pallas_call(
        half_kernel,
        out_shape=jax.ShapeDtypeStruct((4, rows, wide), BF),
        grid_spec=pltpu.PrefetchScalarGridSpec(
            num_scalar_prefetch=1,
            grid=(4,),
            in_specs=specs,
            out_specs=pl.BlockSpec((1, rows, wide), lambda k, place: (k, 0, 0)),
        ),
        compiler_params=pltpu.CompilerParams(vmem_limit_bytes=48 << 20),
        cost_estimate=cost(rows / 210),
    )(place, *arrays)


def turn_kernel(*refs):
    start = 0
    for block in refs[:-1]:
        rows = block.shape[0]
        refs[-1][:, pl.ds(start, rows)] = block[...].T
        start += rows


def turn(*blocks):
    width = blocks[0].shape[1]
    step = 512 if width % 512 == 0 else width
    rows = sum(block.shape[0] for block in blocks)
    return pl.pallas_call(
        turn_kernel,
        out_shape=jax.ShapeDtypeStruct((width, rows), BF),
        grid=(width // step,),
        in_specs=[pl.BlockSpec((block.shape[0], step), lambda i: (0, i)) for block in blocks],
        out_specs=pl.BlockSpec((step, rows), lambda i: (i, 0)),
        compiler_params=pltpu.CompilerParams(vmem_limit_bytes=32 << 20),
        cost_estimate=cost(3),
    )(*blocks)


def turn_own_kernel(place, *refs):
    blocks, out_ref = refs[:-1], refs[-1]
    rows = blocks[0].shape[0]
    for k, block in enumerate(blocks):
        turned = block[...].T
        for r in range(GROUP):
            out_ref[r, :, pl.ds((k ^ r) * rows, rows)] = turned


def turn_own(place, blocks, width):
    rows = blocks[0].shape[0]
    out = (GROUP, width, GROUP * rows)
    return pl.pallas_call(
        turn_own_kernel,
        out_shape=jax.ShapeDtypeStruct(out, BF),
        grid_spec=pltpu.PrefetchScalarGridSpec(
            num_scalar_prefetch=1,
            grid=(1,),
            in_specs=[pl.BlockSpec((rows, width), lambda i, place: (0, place[0]))] * GROUP,
            out_specs=pl.BlockSpec(out, lambda i, place: (0, 0, 0)),
        ),
        compiler_params=pltpu.CompilerParams(vmem_limit_bytes=32 << 20),
        cost_estimate=cost(3),
    )(place, *blocks)


def join_kernel(place, *refs):
    for r, block in enumerate(refs[:-1]):

        @pl.when(pl.program_id(0) == r)
        def _():
            refs[-1][...] = block[...]


def join(place, blocks):
    rows, width = blocks[0].shape
    return pl.pallas_call(
        join_kernel,
        out_shape=jax.ShapeDtypeStruct((GROUP * rows, width), BF),
        grid_spec=pltpu.PrefetchScalarGridSpec(
            num_scalar_prefetch=1,
            grid=(GROUP,),
            in_specs=[fixed(block) for block in blocks],
            out_specs=pl.BlockSpec((rows, width), lambda i, place: (place[0] ^ i, 0)),
        ),
        compiler_params=pltpu.CompilerParams(vmem_limit_bytes=40 << 20),
        cost_estimate=cost(5),
    )(place, *blocks)


def all_grads(parts, terms):
    rows = sum(left.shape[0] for left, right in terms)
    wide = terms[0][1].shape[1] // parts
    specs = []
    for left, right in terms:
        specs.append(pl.BlockSpec(left.shape, lambda p, place: (0, 0)))
        specs.append(pl.BlockSpec((right.shape[0], wide), lambda p, place: (0, p)))
    return pl.pallas_call(
        half_kernel,
        out_shape=jax.ShapeDtypeStruct((parts, rows, wide), BF),
        grid_spec=pltpu.PrefetchScalarGridSpec(
            num_scalar_prefetch=1,
            grid=(parts,),
            in_specs=specs,
            out_specs=pl.BlockSpec((1, rows, wide), lambda p, place: (p, 0, 0)),
        ),
        compiler_params=pltpu.CompilerParams(vmem_limit_bytes=48 << 20),
        cost_estimate=cost(18),
    )(jnp.zeros((2,), jnp.int32), *[array for term in terms for array in term])


def after(values, *earlier):
    return lax.optimization_barrier((values, *earlier))[0]


def wide_sum(*terms):
    total = terms[0].astype(F32)
    for term in terms[1:]:
        total = total + term.astype(F32)
    return total


def solution(mesh):
    dp, fsdp = mesh.shape["dp"], mesh.shape["fsdp"]
    assert fsdp == GROUP and dp % GROUP == 0
    inner = dp // GROUP

    def swap(values, r):
        return lax.ppermute(values, "fsdp", [(i, i ^ r) for i in range(fsdp)])

    def across(values):
        return lax.ppermute(values, "dp", [(i, i ^ 1) for i in range(dp)])

    def gather_blocks(values, chip=None):
        chip = swap(values, 2) if chip is None else chip
        return values, swap(values, 1), chip, swap(chip, 1)

    def gather_rows(values, chip=None):
        return jnp.concatenate(gather_blocks(values, chip), axis=0)

    def core_sum(terms):
        blocks = terms.reshape((GROUP, -1) + terms.shape[1:])
        got = swap(low(blocks[1::2]), 1)
        return wide_sum(blocks[0], got[0]), low(wide_sum(blocks[2], got[1]))

    def scatter_sum(terms):
        own, other = core_sum(terms)
        return own + swap(other, 2).astype(F32)

    def gather_plane(values, near=None):
        half = values.shape[0] // 2
        chip, side = near or (swap(values, 2), across(values))
        far = jnp.concatenate([across(chip[:half]), swap(side[half:], 2)], axis=0)
        blocks = [values, chip, side, far]
        mates = [swap(block, 1) for block in blocks]
        return jnp.concatenate([b for pair in zip(blocks, mates) for b in pair], axis=0)

    def plane_core(terms):
        blocks = terms.reshape((2 * GROUP, -1) + terms.shape[1:])
        got = swap(low(blocks[1::2]), 1)
        return [wide_sum(blocks[2 * i], got[i]) for i in range(GROUP)]

    def plane_far(sums):
        own, chip, side, far = sums
        half = far.shape[0] // 2
        top, bottom = across(low(far[:half])), swap(low(far[half:]), 2)
        chip = jnp.concatenate([wide_sum(chip[:half], top), chip[half:]], axis=0)
        side = jnp.concatenate([side[:half], wide_sum(side[half:], bottom)], axis=0)
        return own, low(chip), low(side)

    def plane_near(sums):
        own, chip, side = sums
        return own, swap(chip, 2), across(side)

    def pick(bit, low_part, high_part, axis):
        return jnp.where(
            bit == 0,
            jnp.concatenate([low_part, high_part], axis=axis),
            jnp.concatenate([high_part, low_part], axis=axis),
        )

    def sent_parts(weights, f, place, parts):
        rows, width = weights[0].shape[0], weights[0].shape[1] // GROUP
        size = rows // parts

        def part(weight, r):
            return lax.dynamic_slice(weight, (place * size, (f ^ r) * width), (size, width))

        return jnp.stack([jnp.stack([part(weight, 2), part(weight, 3)]) for weight in weights])

    def mate_parts(weights, f):
        rows, width = weights[0].shape[0], weights[0].shape[1] // GROUP
        sent = [lax.dynamic_slice(w, (0, (f ^ 1) * width), (rows, width)) for w in weights]
        return swap(jnp.stack(sent), 1)

    def head_pieces(weights, near, far, mate, mate_at=0):
        near_mate, far_mate = swap(near[:, 1], 1), swap(far[:, 1], 1)
        return [
            (
                weight,
                (mate, (i + mate_at,)),
                (near, (i, 0)),
                (far, (i, 0)),
                (near_mate, (i,)),
                (far_mate, (i,)),
            )
            for i, weight in enumerate(weights)
        ]

    def plain_sum(terms):
        parts = []
        for kind, left, right in terms:
            if kind == "owners":
                f = lax.axis_index("fsdp")
                size = left.shape[-2]
                right = right[0][:, :, right[1] * size : (right[1] + 1) * size]
                part = jnp.einsum("srt,stc->src", left, right, preferred_element_type=F32)
                part = jnp.take(part, f ^ jnp.arange(GROUP), axis=0)
                part = part.reshape(GROUP, size, inner, -1).transpose(0, 2, 1, 3)
                parts.append(low(part).reshape((dp, size, -1)))
            elif kind == "columns":
                tall = left.reshape(GROUP, -1, left.shape[1])
                wide = right.reshape(right.shape[0], inner, -1)
                part = jnp.einsum("zrt,txc->zxrc", tall, wide, preferred_element_type=F32)
                parts.append(low(part).reshape((dp,) + part.shape[2:]))
            else:
                wide = right.reshape(right.shape[0], dp, -1)
                parts.append(low(jnp.einsum("rt,tpc->prc", left, wide, preferred_element_type=F32)))
        grads = jnp.concatenate(parts, axis=1)
        return lax.psum_scatter(grads, "dp", scatter_dimension=0).astype(F32)

    def hop(values, bit):
        return lax.ppermute(values, "dp", [(i, i ^ (1 << bit)) for i in range(dp)])

    class Sum:
        def __init__(self, place, terms, order):
            self.place, self.terms, self.order = place, terms, order

        def send(self):
            if dp == 8:
                self.sent = half_grads(self.place, self.terms, self.order, 1)
            else:
                self.sent = self.total = plain_sum(self.terms)
            return self.sent

        def keep(self, *earlier):
            if dp == 8:
                first = after(self.terms[0][1], *earlier)
                terms = ((self.terms[0][0], first, self.terms[0][2]),) + self.terms[1:]
                self.kept = half_grads(self.place, terms, self.order, 0)
                return self.kept
            return self.sent

        def add(self, stage, *earlier):
            if dp != 8:
                return self.sent
            if stage == 1:
                self.one = after(hop(self.sent, self.order[0]), *earlier)
                self.sent = low(wide_sum(self.kept[2:], self.one[2:]))
                return self.sent
            if stage == 2:
                self.two = after(hop(self.sent, self.order[1]), *earlier)
                self.sent = low(wide_sum(self.kept[1], self.one[1], self.two[1]))
                return self.sent
            three = after(hop(self.sent, self.order[2]), *earlier)
            self.total = wide_sum(self.kept[0], self.one[0], self.two[0], three)
            return self.total

        def parts(self):
            out, at = [], 0
            for kind, left, right in self.terms:
                rows = left.shape[0] // GROUP if kind == "columns" else left.shape[-2]
                out.append(self.total[at : at + rows])
                at += rows
            return out

    def place_columns(values):
        pairs = []
        for z in range(GROUP):
            for x in range(inner):
                for f in range(GROUP):
                    pairs.append(((z * inner + x) * GROUP + f, (f * inner + x) * GROUP + z))
        return lax.ppermute(values, ("dp", "fsdp"), pairs)

    def on_device(
        tokens,
        patches,
        cotangent,
        lengths,
        episode_flags,
        norm_gains,
        w_query,
        w_key,
        w_value,
        w_out,
        c_query,
        c_key,
        c_value,
        c_out,
        patch_proj,
        w_gate,
        w_up,
        w_down,
    ):
        f = lax.axis_index("fsdp")
        x = lax.axis_index("dp") % 2
        z = (lax.axis_index("dp") // 2) % 2
        place = jnp.stack([f, lax.axis_index("dp")]).astype(jnp.int32)
        slot = tokens.shape[1]
        keys = patches.shape[1]
        width = tokens.shape[2] // GROUP
        inputs = tokens[0].astype(F32)
        bucket = jnp.where(
            lengths[0] <= slot // 4,
            slot // 4,
            jnp.where(lengths[0] <= slot // 2, slot // 2, slot),
        )
        live = (jnp.arange(slot, dtype=jnp.int32) < bucket).astype(F32)[:, None]
        grad_out = low(cotangent[0].astype(F32) * live)
        info = jnp.stack([lengths, episode_flags], axis=1)
        chip_info = swap(info, 2)
        w_query, w_key, w_value, inputs, chip_info = lax.optimization_barrier(
            (w_query, w_key, w_value, inputs, chip_info)
        )
        pair_near = swap(sent_parts((w_query, w_key), f, x, 2), 2)
        value_near = swap(sent_parts((w_value,), f, x, 2), 2)
        first = normed(inputs, norm_gains[0])
        first_chip = swap(first, 2)
        pair_far = across(pair_near)
        value_far = across(after(value_near, pair_far))

        rows = patch_proj.shape[0] // 4
        patch_in = after(patch_proj, pair_near)
        patch_mate = swap(patch_in, 1)
        patch_part = swap(lax.dynamic_slice_in_dim(patch_in, (2 * x + z) * rows, rows, 0), 2)
        patch_half = pick(z, patch_part, hop(patch_part, 1), 0)
        patch_chip = pick(x, patch_half, across(patch_half), 0)
        patch_far = swap(patch_chip, 1)
        cross_own = (c_key, c_value, c_query)
        cross_ready = after(cross_own, patch_part, value_near)
        cross_part = swap(sent_parts(cross_ready, f, 2 * x + z, 4), 2)
        cross_near = pick(z, cross_part, hop(cross_part, 1), 2)
        cross_far = across(cross_near)
        self_mate = mate_parts((w_query, w_key, w_value), f)
        first_blocks = gather_blocks(first, after(first_chip, pair_far))
        info = jnp.concatenate([info, swap(info, 1), chip_info, swap(chip_info, 1)], axis=0)
        query_w, key_w = head_pieces((w_query, w_key), pair_near, pair_far, self_mate)
        (value_w,) = head_pieces((w_value,), value_near, value_far, self_mate, 2)
        queries = to_heads(place, first_blocks, query_w)
        keys_all = to_heads(place, first_blocks, key_w)
        values_all = to_heads(place, first_blocks, value_w)
        mixed = attend(info, queries, keys_all, values_all, slot, slot, width, True)
        own, other = core_sum(low(nn(after(mixed, cross_near, patch_half), w_out)))
        cross_mate = mate_parts(after(cross_own, other), f)
        sent_out = other
        other = swap(other, 2)
        after_self = inputs + own + other.astype(F32)
        second = normed(after_self, norm_gains[1])
        second_chip = swap(second, 2)
        patch_blocks = (patch_proj, patch_mate, patch_chip, patch_far)
        patch_mat = join(place, after(patch_blocks, sent_out))
        context = low(nn(after(patches[0], second), patch_mat))
        context_chip = swap(context, 2)
        second_chip, cross_far = lax.optimization_barrier((second_chip, cross_far))
        second_blocks = gather_blocks(second, second_chip)
        cross_key_w, cross_value_w, cross_query_w = head_pieces(
            cross_own, cross_near, cross_far, cross_mate
        )
        cross_q = to_heads(place, second_blocks, cross_query_w)
        context_blocks = gather_blocks(context, after(context_chip, cross_q))
        cross_k = to_heads(place, context_blocks, cross_key_w)
        cross_v = to_heads(place, context_blocks, cross_value_w)
        cross_mixed = attend(info, cross_q, cross_k, cross_v, slot, keys, width, False)
        grad_early = after(grad_out, context)
        cross_mixed, *grad_near = lax.optimization_barrier(
            (cross_mixed, swap(grad_early, 2), across(grad_early))
        )
        own, other = core_sum(low(nn(cross_mixed, c_out)))
        grad_all = gather_plane(grad_out, tuple(grad_near))
        other = after(swap(other, 2), grad_all)
        after_cross = after_self + own + other.astype(F32)
        third = normed(after_cross, norm_gains[2])
        third_all = gather_plane(third)
        patch_width = patch_proj.shape[0]
        patch_rows = after(patches[0], third_all)

        def patch_piece(r):
            return lax.dynamic_slice(patch_rows, (0, (f ^ r) * patch_width), (keys, patch_width))

        patch_pieces = [patch_piece(0)] + [swap(patch_piece(r), r) for r in range(1, GROUP)]

        units = w_gate.shape[0] // 2
        gate_half, up_half, down_half = (
            lax.dynamic_slice_in_dim(w, x * units, units, 0) for w in (w_gate, w_up, w_down)
        )
        gate = nt(third_all, gate_half)
        up = nt(third_all, up_half)
        value, slope = gelu_parts(gate)
        hidden = low(value * up)
        grad_hidden = nt(grad_all, down_half)
        grad_gate = low(grad_hidden * up * slope)
        grad_up = low(grad_hidden * value)
        grad_gate, *patch_pieces = lax.optimization_barrier((grad_gate, *patch_pieces))
        third_part = low(nn(grad_gate, gate_half) + nn(grad_up, up_half))
        sums = plane_far(plane_core(third_part))
        hidden_terms = tuple(
            (turn(after(left, third_part)), right)
            for left, right in ((grad_gate, third_all), (grad_up, third_all), (hidden, grad_all))
        )
        first_left = after(hidden_terms[0][0], sums[1], sums[2])
        hidden_terms = ((first_left, third_all),) + hidden_terms[1:]
        hidden_bundle = all_grads(dp // 2, hidden_terms)
        hidden_grads = lax.psum_scatter(
            hidden_bundle,
            "dp",
            scatter_dimension=0,
            axis_index_groups=[list(range(i, dp, 2)) for i in range(2)],
        )
        own, chip, side = plane_near(sums)
        grad_third = wide_sum(own, after(chip, hidden_bundle), side)

        grad_norm, gain_third = norm_back(after_cross, norm_gains[2], grad_third)
        grad_after_cross = grad_out.astype(F32) + grad_norm
        grad_cross_out = low(grad_after_cross)
        cross_turned = turn(after(cross_mixed, grad_third))
        second_turned = turn(*after(second_blocks, grad_third))
        grad_cross_all = gather_rows(
            grad_cross_out, after(swap(grad_cross_out, 2), cross_turned, second_turned)
        )
        grad_cross_mixed = low(nt(grad_cross_all, c_out))
        grad_cq, grad_ck, grad_cv = attend_back(
            info, cross_q, cross_k, cross_v, grad_cross_mixed, slot, keys, width, False
        )
        own, other = core_sum(from_heads(place, (grad_cq,), (cross_query_w,)))
        context_turned = turn(*after(context_blocks, grad_cq))
        sum_cross = Sum(
            place,
            (("rows", cross_turned, grad_cross_all), ("columns", second_turned, grad_cq)),
            (0, 1, 2),
        )
        grad_second = own + after(swap(other, 2), sum_cross.send(), context_turned).astype(F32)

        grad_norm, gain_second = norm_back(after_self, norm_gains[1], grad_second)
        grad_after_self = grad_after_cross + grad_norm
        grad_self_out = low(grad_after_self)
        self_chip = swap(grad_self_out, 2)
        mixed_turned = turn(after(mixed, grad_self_out))
        first_turned = turn_own(place, after(first_blocks, grad_self_out), width)
        grad_self_all = gather_rows(
            grad_self_out,
            after(self_chip, mixed_turned, first_turned, sum_cross.keep(grad_self_out)),
        )
        grad_mixed = low(nt(grad_self_all, w_out))
        grad_q, grad_k, grad_v = attend_back(
            info, queries, keys_all, values_all, grad_mixed, slot, slot, width, True
        )
        heads = jnp.concatenate([grad_q, grad_k, grad_v], axis=1)
        heads_chip = swap(heads, 2)
        self_part = from_heads(place, (grad_q, grad_k, grad_v), (query_w, key_w, value_w))
        own, other = core_sum(self_part)
        other = swap(other, 2)
        context_part = from_heads(
            place, (after(grad_ck, self_part), grad_cv), (cross_key_w, cross_value_w)
        )
        context_own, context_other = core_sum(context_part)
        context_other = swap(context_other, 2)
        cross_one = sum_cross.add(1, context_part)
        sum_context = Sum(
            place,
            (
                ("columns", context_turned, grad_ck),
                ("columns", context_turned, grad_cv),
                ("rows", after(mixed_turned, heads_chip), grad_self_all),
            ),
            (0, 1, 2),
        )
        grad_first = own + after(
            other, sum_context.send(), cross_one, hidden_grads
        ).astype(F32)
        grad_norm, gain_first = norm_back(inputs, norm_gains[0], grad_first)
        tokens_grad = (grad_after_self + grad_norm)[None]
        gains = jnp.stack([gain_first, gain_second, gain_third])
        heads_all = jnp.stack([heads, swap(heads, 1), heads_chip, swap(heads_chip, 1)])
        sum_self = Sum(
            place,
            (("owners", first_turned, (heads_all, 0)), ("owners", first_turned, (heads_all, 1))),
            (0, 1, 2),
        )
        sum_value = Sum(place, (("owners", first_turned, (heads_all, 2)),), (1, 0, 2))
        kept = sum_context.keep(sum_self.send(), sum_value.send())
        step = sum_cross.add(2, kept)
        patch_turned = turn(*after(tuple(patch_pieces), kept))
        grad_context = low(context_own + after(context_other, kept, patch_turned).astype(F32))
        context_chip = swap(grad_context, 2)
        for bit in reversed(range(2, dp.bit_length() - 1)):
            gains = gains + after(hop(gains, bit), patch_turned)
        gains = gains + after(hop(gains, 1), grad_context)
        kept = sum_self.keep(grad_context, gains), sum_value.keep(grad_context)
        value_one = sum_value.add(1, *kept)
        context_chip = after(context_chip, value_one, step)
        grad_context_all = gather_rows(grad_context, context_chip)
        sum_patch = Sum(place, (("rows", patch_turned, grad_context_all),), (1, 0, 2))
        sum_patch.send()
        kept = sum_patch.keep(sum_patch.sent)
        patch_one = sum_patch.add(1, kept)
        context_one = sum_context.add(1, patch_one)
        out_part = low(nn(after(hidden, context_one), down_half))
        sums = plane_core(out_part)
        patches_grad = nt(after(grad_context, context_one), patch_mat)[None]
        step = sum_cross.add(3, out_part, patches_grad)
        step = sum_context.add(2, step)
        step = sum_self.add(1, step)
        own, chip, side = plane_far(after(tuple(sums), step))
        step = sum_value.add(2, step)
        gains = gains + after(hop(after(gains, step), 0), chip, side)
        gains = gains + after(swap(gains, 2), chip)
        gains_grad = gains + after(swap(gains, 1), chip)
        step = sum_patch.add(2, step, chip, side, gains_grad)
        step = sum_self.add(2, step)
        columns = tokens.shape[2] // dp
        hidden_grads = after(hidden_grads, step)
        hidden_other = across(
            lax.dynamic_slice_in_dim(hidden_grads, (1 - x) * columns, columns, 1)
        )
        own, chip, side = plane_near((own, chip, side))
        step = sum_context.add(3, step)
        c_out_grad, c_query_grad = sum_cross.parts()
        c_key_grad, c_value_grad, w_out_grad = sum_context.parts()
        moved = place_columns(low(jnp.stack([c_query_grad, c_key_grad, c_value_grad])))
        step = sum_value.add(3, step, hidden_other)
        step = sum_self.add(3, step)
        out_tokens = low((after_cross + wide_sum(own, after(chip, step), side)) * live)[None]
        hidden_mine = lax.dynamic_slice_in_dim(hidden_grads, x * columns, columns, 1)
        hidden_mine, hidden_other = after((hidden_mine, hidden_other), step)

        def both_halves(i):
            mine, other = (
                half[i * units : (i + 1) * units] for half in (hidden_mine, hidden_other)
            )
            return jnp.where(
                x == 0,
                jnp.concatenate([mine, other], axis=0),
                jnp.concatenate([other, mine], axis=0),
            ).astype(F32)

        gate_grad, up_grad, down_grad = (both_halves(i) for i in range(3))
        step = sum_patch.add(3, step, gate_grad)
        c_query_grad, c_key_grad, c_value_grad = after(moved, step).astype(F32)

        w_query_grad, w_key_grad = sum_self.parts()
        (w_value_grad,), (patch_proj_grad,) = sum_value.parts(), sum_patch.parts()

        return (
            out_tokens,
            tokens_grad,
            patches_grad,
            gains_grad,
            w_query_grad,
            w_key_grad,
            w_value_grad,
            w_out_grad,
            c_query_grad,
            c_key_grad,
            c_value_grad,
            c_out_grad,
            patch_proj_grad,
            gate_grad,
            up_grad,
            down_grad,
        )

    both, rows, block = ("dp", "fsdp"), P("fsdp", None), P("fsdp", "dp")
    whole = P(both, None, None)
    return jax.shard_map(
        on_device,
        mesh=mesh,
        in_specs=(whole, whole, whole, P(both), P(both), P()) + (rows,) * 12,
        out_specs=(whole, whole, whole, P()) + (block,) * 12,
        check_vma=False,
    )
```
